32 devices in a mesh: dp: 8 (over y, x, core), feat: 4 (over z).
Axes of the slice: x: 2, y: 2, z: 4, core: 2. Of those that a mesh axis runs over, the one named last changes fastest.
Arguments:
- inputs: float32 [4096, 2048], P('dp', 'feat'), may hold values from -6 to 6
- partner_bits: int32 [4, 2], P('feat'), may hold values from 0 to 1, each once within a row
- block_weights: float32 [4, 512, 3, 512], P('feat', 'dp'), may hold values from -0.15625 to 0.15625
- low_left: float32 [4, 512, 256], P('feat', 'dp'), may hold values from -0.125 to 0.125
- low_right: float32 [4, 256, 512], P('feat', 'dp'), may hold values from -0.375 to 0.375
- cotangent: float32 [4096, 2048], P('dp', 'feat'), may hold values from -6 to 6
Outputs:
- outputs: float32 [4096, 2048], P('dp', 'feat')
- input_grad: float32 [4096, 2048], P('dp', 'feat')
- block_grads: float32 [4, 512, 3, 512], P('feat', 'dp')
- left_grads: float32 [4, 512, 256], P('feat', 'dp')
- right_grads: float32 [4, 256, 512], P('feat', 'dp')
The draws below stay inside these ranges and needn't reach their ends.
Inputs may be any that keep to these rules, and one draw needn't show every extreme that they name: `partner_bits`: each row holds every bit number 0 .. 1 once.
All inputs are finite; a program needn't handle non-finite values.
Results may differ from the reference program's by a relative error of at most 0.000086.
Values sent between devices are 32-bit elements; how exact they have to be, the bound alone decides.
No kernel may reach another device: no remote copies, remote signals or barrier semaphores. Data moves between devices by JAX's collectives and lax.ppermute only.
A program may use at most 128 MiB of HBM per device.

```python
import jax
import jax.numpy as jnp
from jax import lax

BLOCK = 512
LOWRANK = 256
SECTIONS = 2
WIDTH = 2048
TOKENS = 4096
N_FEAT = 4


def steps_of(own_key, shape, cuts, low, top_value):
    def one(position, shards_of):
        draws = jax.random.uniform(jax.random.fold_in(jax.random.fold_in(own_key, 6), position), (shards_of,), jnp.float32, low / len(cuts), top_value / len(cuts))
        return jnp.repeat(jnp.exp(draws), shape[position] // shards_of).reshape((-1,) + (1,) * (len(shape) - position - 1))

    loudness = one(*cuts[0])
    for cut in cuts[1:]:
        loudness = loudness * one(*cut)
    return loudness


def scatter_about(own_key, dims, scale, limit, split=(), kind=jnp.bfloat16):
    gain = steps_of(own_key, dims, split, -0.22, 0.18) if split else 1.0
    entries = jax.random.normal(own_key, dims, jnp.float32) * scale * gain
    return jnp.minimum(jnp.maximum(entries, -limit), limit).astype(kind)


def setup_inputs(seed: int = 0) -> dict:
    keys = jax.random.split(jax.random.key(seed), 7)
    inputs = scatter_about(keys[0], (TOKENS, WIDTH), 1.0, 6.0, ((0, 8), (1, 4)), jnp.float32)
    partner_bits = jax.vmap(lambda own: jax.random.permutation(own, SECTIONS))(jax.random.split(keys[1], N_FEAT)).reshape((N_FEAT, SECTIONS)).astype(jnp.int32)
    block_weights = scatter_about(keys[2], (N_FEAT, BLOCK, SECTIONS + 1, BLOCK), ((SECTIONS + 1) * BLOCK) ** -0.5, 0.15625, ((0, 4), (1, 8)), jnp.float32)
    low_left = scatter_about(keys[3], (N_FEAT, BLOCK, LOWRANK), WIDTH ** -0.5, 0.125, ((0, 4), (1, 8)), jnp.float32)
    low_right = scatter_about(keys[4], (N_FEAT, LOWRANK, BLOCK), LOWRANK ** -0.5, 0.375, ((0, 4), (1, 8)), jnp.float32)
    cotangent = scatter_about(keys[5], (TOKENS, WIDTH), 1.0, 6.0, ((0, 8), (1, 4)), jnp.float32)
    return {"inputs": inputs, "partner_bits": partner_bits, "block_weights": block_weights, "low_left": low_left, "low_right": low_right, "cotangent": cotangent}


def forward(inputs, block_weights, low_left, low_right, partner_bits):
    highest = lax.Precision.HIGHEST
    blocked = inputs.reshape(TOKENS, N_FEAT, BLOCK)
    owners = jnp.arange(N_FEAT, dtype=jnp.int32)
    others = jnp.bitwise_xor(owners[:, None], jnp.left_shift(jnp.ones_like(partner_bits), partner_bits))
    sources = jnp.concatenate([owners[:, None], others], axis=1).astype(jnp.int32)
    gathered = blocked[:, sources, :]
    sparse = jnp.einsum('tjsi,jiso->tjo', gathered, block_weights, precision=highest)
    codes = jnp.einsum('tji,jir->tr', blocked, low_left, precision=highest)
    lowpart = jnp.einsum('tr,jro->tjo', codes, low_right, precision=highest)
    return (sparse + lowpart).reshape(TOKENS, WIDTH)

def reference(inputs, partner_bits, block_weights, low_left, low_right, cotangent):

    def layer(first, second, third, fourth):
        return forward(first, second, third, fourth, partner_bits)
    outputs, pullback = jax.vjp(layer, inputs, block_weights, low_left, low_right)
    grads = pullback(cotangent)
    scale = 1.0 / jnp.sqrt(jnp.float32(TOKENS))
    return (outputs, grads[0], grads[1] * scale, grads[2] * scale, grads[3] * scale)
```

```python
import functools
import math

import jax
import jax.numpy as jnp
from jax import lax
from jax.experimental import pallas as pl
from jax.experimental.pallas import tpu as pltpu
from jax.sharding import PartitionSpec as P

F32 = jnp.float32
BF16 = jnp.bfloat16
VMEM_BYTES = 40 * 1024 * 1024
TOKEN_BLOCK = 256


def across(block, axis, apart):
    count = lax.axis_size(axis)
    return lax.ppermute(block, axis, [(i, i ^ apart) for i in range(count)])


def split(value):
    high = value.astype(BF16)
    return high, (value - high.astype(F32)).astype(BF16)


def dot3(left, right, over):
    def one(a, b):
        return lax.dot_general(
            a, b, ((over[:1], over[1:]), ((), ())), preferred_element_type=F32
        )

    return one(left[0], right[0]) + (one(left[0], right[1]) + one(left[1], right[0]))


def nn(left, right):
    return dot3(left, right, (1, 0))


def nt(left, right):
    return dot3(left, right, (1, 1))


def tn(left, right):
    return dot3(left, right, (0, 0))


def call(kernel, out_shapes, operands, grid=None, in_specs=None, out_specs=None, scratch=()):
    vmem = pl.BlockSpec(memory_space=pltpu.VMEM)
    kwargs = {}
    if grid is None:
        in_specs = in_specs or [vmem] * len(operands)
        out_specs = [vmem] * len(out_shapes)
    else:
        kwargs["grid"] = grid
    return pl.pallas_call(
        kernel,
        out_shape=out_shapes,
        in_specs=in_specs,
        out_specs=out_specs,
        scratch_shapes=list(scratch),
        cost_estimate=pl.CostEstimate(flops=1, bytes_accessed=1, transcendentals=0),
        compiler_params=pltpu.CompilerParams(vmem_limit_bytes=VMEM_BYTES),
        **kwargs,
    )(*operands)


def f32(*shape):
    return jax.ShapeDtypeStruct(shape, F32)


def b16(*shape):
    return jax.ShapeDtypeStruct(shape, BF16)


def whole(shape):
    return pl.BlockSpec(shape, lambda *_: (0,) * len(shape))


def by_tokens(tokens, width):
    return pl.BlockSpec((tokens, width), lambda i: (i, 0))


def slot_weights(bits_ref, w_ref, bit, sections):
    chosen = w_ref[0, sections]
    for s in range(sections - 1):
        chosen = jnp.where(bits_ref[0, s] == bit, w_ref[0, 1 + s], chosen)
    return chosen


def put_left(out_ref, left, block):
    rows, rank = left.shape
    pieces = block // rank
    step = rows // pieces
    for p in range(pieces):
        out_ref[:step, p * rank : (p + 1) * rank] = left[p * step : (p + 1) * step]


def pack_kernel(bits_ref, w_ref, left_ref, right_ref, x_ref, g_ref, near_ref, far_ref, own_ref):
    _, slots, rows, block = w_ref.shape
    sections = slots - 1
    rank_rows = right_ref.shape[1]
    flat = far_ref.shape[0] - x_ref.shape[0]
    near_ref[:rows] = slot_weights(bits_ref, w_ref, 0, sections)
    near_ref[rows : rows + rank_rows] = right_ref[0]
    near_ref[rows + rank_rows :] = g_ref[...]
    put_left(far_ref.at[:flat], left_ref[0], block)
    far_ref[flat:] = x_ref[...]
    own_ref[:rows] = w_ref[0, 0]
    for b in range(1, sections):
        own_ref[b * rows : (b + 1) * rows] = slot_weights(bits_ref, w_ref, b, sections)
    at = sections * rows
    own_ref[at : at + rank_rows] = right_ref[0]
    put_left(own_ref.at[at + rank_rows :], left_ref[0], block)


def before_kernel(sizes, *refs):
    sections, rows, rank_rows, rank, dp_count = sizes
    even_ref, odd_ref, x_ref, g_ref = refs[:4]
    wh, wl, rh, rl, lh, ll, c_ref, cg_ref, ahead_ref, *back_refs = refs[4:]
    block = x_ref.shape[1]
    flat = rows * rank // block
    pieces = rows // flat

    @pl.when(pl.program_id(0) == 0)
    def _():
        me = lax.axis_index("dp")
        for k in range(dp_count):
            part = (odd_ref if k % 2 else even_ref).at[k // 2]
            owner = me ^ k
            at = 0

            def move(high_ref, low_ref, i, start, count, value):
                high, low = split(value)
                place = pl.ds(pl.multiple_of(start, 16), count)
                high_ref[i, place, :] = high
                low_ref[i, place, :] = low

            def move_wide(high_ref, low_ref, i, start, count):
                move(high_ref, low_ref, i, owner * count, count, part[start : start + count, :])
                return start + count

            def move_left(i, start):
                for p in range(pieces):
                    value = part[start : start + flat, p * rank : (p + 1) * rank]
                    move(lh, ll, i, owner * rows + p * flat, flat, value)
                return start + flat

            for i in range(sections):
                at = move_wide(wh, wl, i, at, rows)
            at = move_wide(rh, rl, 0, at, rank_rows)
            at = move_left(0, at)
            at = move_wide(wh, wl, sections, at, rows)
            at = move_wide(rh, rl, 1, at, rank_rows)
            at = move_left(1, at)

    x, g = split(x_ref[...]), split(g_ref[...])
    c_ref[...] = nn(x, (lh[0], ll[0]))
    cg_ref[...] = nt(g, (rh[0], rl[0]))
    ahead_ref[...] = nn(x, (wh[sections], wl[sections]))
    for b in range(1, sections):
        back_refs[b - 1][...] = nt(g, (wh[b], wl[b]))


def codes_kernel(far_ref, near_ref, lh, ll, rh, rl, c0_ref, cg0_ref, c_ref, cg_ref):
    c_ref[...] = c0_ref[...] + nn(split(far_ref[...]), (lh[1], ll[1]))
    cg_ref[...] = cg0_ref[...] + nt(split(near_ref[...]), (rh[1], rl[1]))


def send_kernel(lh, ll, rh, rl, c_ref, cg_ref, back0_ref, ahead0_ref, back_ref, ahead_ref):
    back_ref[...] = back0_ref[...] + nt(split(cg_ref[...]), (lh[1], ll[1]))
    ahead_ref[...] = ahead0_ref[...] + nn(split(c_ref[...]), (rh[1], rl[1]))


def codes_send_kernel(
    far_ref, near_ref, lh, ll, rh, rl, c0_ref, cg0_ref, back0_ref, ahead0_ref,
    c_ref, cg_ref, back_ref, ahead_ref,
):
    codes_kernel(far_ref, near_ref, lh, ll, rh, rl, c0_ref, cg0_ref, c_ref, cg_ref)
    send_kernel(lh, ll, rh, rl, c_ref, cg_ref, back0_ref, ahead0_ref, back_ref, ahead_ref)


def grads_kernel(sizes, scale, *refs):
    sections, rows, rank_rows, rank, dp_count = sizes
    x_ref, g_ref, near_ref, c_ref, cg_ref, *rest = refs
    far_refs = rest[: sections - 1]
    half = dp_count // 2
    keep_refs = rest[sections - 1 : sections - 1 + half]
    give_ref = rest[sections - 1 + half]
    dw, dr, dl = rest[sections + half :]
    block = x_ref.shape[1]
    flat = rows * rank // block
    pieces = rows // flat
    me = lax.axis_index("dp")
    at = [0]

    def spread(count, read):
        for k in range(dp_count):
            place = pl.ds(pl.multiple_of((me ^ k) * count, 8), count)
            if k % 2:
                read(give_ref.at[k // 2], at[0], place)
            else:
                read(keep_refs[k // 2], at[0], place)

    def spread_wide(source, count):
        def read(out, start, place):
            out[start : start + count, :] = source[place, :]

        spread(count, read)
        at[0] += count

    def spread_left(source):
        def read(out, start, place):
            value = source[place, :]
            for p in range(pieces):
                out[start : start + flat, p * rank : (p + 1) * rank] = value[
                    p * flat : (p + 1) * flat
                ]

        spread(rows, read)
        at[0] += flat

    x, g, near = split(x_ref[...]), split(g_ref[...]), split(near_ref[...])
    c, cg = split(c_ref[...]), split(cg_ref[...])
    far = [split(r[...]) for r in far_refs]
    dw[...] = tn(x, near) * scale
    spread_wide(dw, rows)
    dr[...] = tn(c, near) * scale
    spread_wide(dr, rank_rows)
    dl[...] = tn(far[0], cg) * scale
    spread_left(dl)
    dw[...] = tn(x, g) * scale
    spread_wide(dw, rows)
    for b in range(1, sections):
        dw[...] = tn(far[b - 1], g) * scale
        spread_wide(dw, rows)
    dr[...] = tn(c, g) * scale
    spread_wide(dr, rank_rows)
    dl[...] = tn(x, cg) * scale
    spread_left(dl)


def local_kernel(sections, *refs):
    x_ref, g_ref, near_ref, c_ref, cg_ref, *rest = refs
    far_refs = rest[: sections - 1]
    wh, wl, rh, rl, lh, ll, out_ref, grad_ref = rest[sections - 1 :]
    out = nn(split(x_ref[...]), (wh[0], wl[0])) + nn(split(c_ref[...]), (rh[0], rl[0]))
    for b in range(1, sections):
        out += nn(split(far_refs[b - 1][...]), (wh[b], wl[b]))
    out_ref[...] = out
    grad = nt(split(g_ref[...]), (wh[0], wl[0])) + nt(split(cg_ref[...]), (lh[0], ll[0]))
    grad_ref[...] = grad + nt(split(near_ref[...]), (wh[sections], wl[sections]))


def place_kernel(sizes, *refs):
    sections, rows, rank_rows, rank, _ = sizes
    bits_ref, kept_ref, near_ref, far_ref, w_ref, left_ref, right_ref = refs
    block = kept_ref.shape[1]
    flat = rows * rank // block
    pieces = rows // flat
    w_ref[0, 0] = kept_ref[:rows]
    for s in range(sections):
        chosen = near_ref[:rows]
        for b in range(1, sections):
            chosen = jnp.where(bits_ref[0, s] == b, kept_ref[b * rows : (b + 1) * rows], chosen)
        w_ref[0, 1 + s] = chosen
    at = sections * rows
    right_ref[0] = kept_ref[at : at + rank_rows] + near_ref[rows:]
    at += rank_rows
    for p in range(pieces):
        columns = slice(p * rank, (p + 1) * rank)
        left_ref[0, p * flat : (p + 1) * flat, :] = (
            kept_ref[at : at + flat, columns] + far_ref[:, columns]
        )


def on_device(inputs, partner_bits, block_weights, low_left, low_right, cotangent):
    tokens, block = inputs.shape
    sections = partner_bits.shape[1]
    dp_count = lax.axis_size("dp")
    half = dp_count // 2
    rows, rank = low_left.shape[1:]
    rank_rows = low_right.shape[1]
    all_rank = rank_rows * dp_count
    flat = rows * rank // block
    sizes = (sections, rows, rank_rows, rank, dp_count)
    step = min(tokens, TOKEN_BLOCK)
    grid = (tokens // step,)
    smem = pl.BlockSpec(memory_space=pltpu.SMEM)
    vmem = pl.BlockSpec(memory_space=pltpu.VMEM)

    lent_rows = rows + rank_rows
    early = tokens // 4
    by_slot = jnp.transpose(block_weights, (0, 2, 1, 3))
    own_rows = sections * rows + rank_rows + flat
    out_near, out_far, own = call(
        pack_kernel,
        [f32(lent_rows + early, block), f32(flat + early, block), f32(own_rows, block)],
        [partner_bits, by_slot, low_left, low_right, inputs, cotangent],
        grid=(1,),
        in_specs=[
            smem, whole(by_slot.shape), whole(low_left.shape), whole(low_right.shape),
            whole((early, block)), whole((early, block)),
        ],
        out_specs=[
            whole((lent_rows + early, block)), whole((flat + early, block)),
            whole((own_rows, block)),
        ],
    )
    got_near = across(out_near, "feat", 1)
    got_far = across(out_far, "feat", 2)
    own = [own] + [across(own, "dp", k) for k in range(2, dp_count, 2)]
    late_x, late_g, got_near, got_far = lax.optimization_barrier(
        (inputs[early:], cotangent[early:], got_near, got_far)
    )
    far = [jnp.concatenate([got_far[flat:], across(late_x, "feat", 2)])]
    far += [across(inputs, "feat", 1 << b) for b in range(2, sections)]
    near = jnp.concatenate([got_near[lent_rows:], across(late_g, "feat", 1)])

    packed_rows = (sections + 1) * rows + 2 * rank_rows + 2 * flat
    w_shape = (sections + 1, block, block)
    r_shape = (2, all_rank, block)
    l_shape = (2, block, rank)
    shapes = [w_shape, w_shape, r_shape, r_shape, l_shape, l_shape]
    wide, thin = by_tokens(step, block), by_tokens(step, rank)
    made = (
        [b16(*s) for s in shapes] + [f32(tokens, rank)] * 2 + [f32(tokens, block)] * sections
    )
    usual = partner_bits[0, 0] >= 0

    def prepare(own, got_near, got_far, inputs, cotangent):
        lent = jnp.concatenate([got_near[:lent_rows], got_far[:flat]])
        lent = [lent] + [across(lent, "dp", k) for k in range(2, dp_count, 2)]
        even = jnp.stack([jnp.concatenate(pair) for pair in zip(own, lent)])
        odd = across(even, "dp", 1)
        return tuple(call(
            functools.partial(before_kernel, sizes),
            [b16(*s) for s in shapes]
            + [f32(tokens, rank)] * 2
            + [f32(tokens, block)] * sections,
            [even, odd, inputs, cotangent],
            grid=grid,
            in_specs=[whole((half, packed_rows, block))] * 2 + [wide, wide],
            out_specs=[whole(s) for s in shapes] + [thin, thin] + [wide] * sections,
        ))

    def empty(*_):
        return tuple(jnp.zeros(s.shape, s.dtype) for s in made)

    wh, wl, rh, rl, lh, ll, codes, code_grads, ahead, *back = lax.cond(
        usual, prepare, empty,
        own, got_near, got_far, inputs, cotangent,
    )
    low_specs = [whole(l_shape), whole(l_shape), whole(r_shape), whole(r_shape)]
    low = [lh, ll, rh, rl]
    if sections == 2:
        codes, code_grads, back[0], ahead = call(
            codes_send_kernel,
            [f32(tokens, rank)] * 2 + [f32(tokens, block)] * 2,
            [far[0], near, *low, codes, code_grads, back[0], ahead],
            grid=grid,
            in_specs=[wide, wide, *low_specs, thin, thin, wide, wide],
            out_specs=[thin, thin, wide, wide],
        )
    else:
        codes, code_grads = call(
            codes_kernel,
            [f32(tokens, rank)] * 2,
            [far[0], near, *low, codes, code_grads],
            grid=grid,
            in_specs=[wide, wide, *low_specs, thin, thin],
            out_specs=[thin, thin],
        )
        for b in range(2, sections):
            codes = codes + across(codes, "feat", 1 << b)
            code_grads = code_grads + across(code_grads, "feat", 1 << b)
        back[0], ahead = call(
            send_kernel,
            [f32(tokens, block)] * 2,
            [*low, codes, code_grads, back[0], ahead],
            grid=grid,
            in_specs=[*low_specs, thin, thin, wide, wide],
            out_specs=[wide, wide],
        )
    back = [across(back[b - 1], "feat", 1 << b) for b in range(1, sections)]
    ahead = across(ahead, "feat", 1)

    scale = 1.0 / math.sqrt(tokens * dp_count)

    def finish(inputs, cotangent, near, codes, code_grads, far, weights):
        *keep, give = call(
            functools.partial(grads_kernel, sizes, scale),
            [f32(packed_rows, block)] * half + [f32(half, packed_rows, block)],
            [inputs, cotangent, near, codes, code_grads, *far],
            scratch=[
                pltpu.VMEM((block, block), F32),
                pltpu.VMEM((all_rank, block), F32),
                pltpu.VMEM((block, rank), F32),
            ],
        )
        codes, code_grads, give = lax.optimization_barrier((codes, code_grads, give))
        got = across(give, "dp", 1)
        summed = [keep[m] + got[m] for m in range(half)]
        total = summed[0]
        for m in range(1, half):
            total = total + across(summed[m], "dp", 2 * m)
        out, grad = call(
            functools.partial(local_kernel, sections),
            [f32(tokens, block)] * 2,
            [inputs, cotangent, near, codes, code_grads, *far, *weights],
            grid=grid,
            in_specs=[wide] * 3 + [thin] * 2 + [wide] * (sections - 1) + [whole(s) for s in shapes],
            out_specs=[wide, wide],
        )
        return out, grad, total[:lent_rows], total[lent_rows : lent_rows + flat], total[lent_rows + flat :]

    def nothing(*_):
        wide_zero = jnp.zeros((tokens, block), F32)
        return (
            wide_zero, wide_zero, jnp.zeros((lent_rows, block), F32),
            jnp.zeros((flat, block), F32), jnp.zeros((packed_rows - lent_rows - flat, block), F32),
        )

    out, grad, near_back, far_back, kept = lax.cond(
        usual, finish, nothing,
        inputs, cotangent, near, codes, code_grads, far, [wh, wl, rh, rl, lh, ll],
    )
    near_back = across(near_back, "feat", 1)
    far_back = across(far_back, "feat", 2)
    block_grads, left_grads, right_grads = call(
        functools.partial(place_kernel, sizes),
        [f32(*by_slot.shape), f32(*low_left.shape), f32(*low_right.shape)],
        [partner_bits, kept, near_back, far_back],
        in_specs=[smem] + [vmem] * 3,
    )
    block_grads = jnp.transpose(block_grads, (0, 2, 1, 3))
    outputs = out + ahead
    for part in back:
        grad = grad + part
    return (outputs, grad, block_grads, left_grads, right_grads)


def solution(mesh):
    in_specs = (
        P("dp", "feat"),
        P("feat", None),
        P("feat", "dp", None, None),
        P("feat", "dp", None),
        P("feat", "dp", None),
        P("dp", "feat"),
    )
    out_specs = (
        P("dp", "feat"),
        P("dp", "feat"),
        P("feat", "dp", None, None),
        P("feat", "dp", None),
        P("feat", "dp", None),
    )
    return jax.shard_map(
        on_device, mesh=mesh, in_specs=in_specs, out_specs=out_specs, check_vma=False
    )
```

```python
import functools
import math

import jax
import jax.numpy as jnp
from jax import lax
from jax.experimental import pallas as pl
from jax.experimental.pallas import tpu as pltpu
from jax.sharding import PartitionSpec as P

F32 = jnp.float32
BF16 = jnp.bfloat16
VMEM_BYTES = 32 * 1024 * 1024
PACK_VMEM_BYTES = 60 * 1024 * 1024


def across(block, axis, apart):
    count = lax.axis_size(axis)
    return lax.ppermute(block, axis, [(i, i ^ apart) for i in range(count)])


def split(value):
    high = value.astype(BF16)
    return high, (value - high.astype(F32)).astype(BF16)


def dot3(left, right, over):
    def one(a, b):
        return lax.dot_general(
            a, b, ((over[:1], over[1:]), ((), ())), preferred_element_type=F32
        )

    return one(left[0], right[0]) + (one(left[0], right[1]) + one(left[1], right[0]))


def nn(left, right):
    return dot3(left, right, (1, 0))


def nt(left, right):
    return dot3(left, right, (1, 1))


def tn(left, right):
    return dot3(left, right, (0, 0))


def call(
    kernel, out_shapes, operands, grid=None, in_specs=None, out_specs=None, scratch=(),
    vmem_bytes=VMEM_BYTES, aliases=None,
):
    vmem = pl.BlockSpec(memory_space=pltpu.VMEM)
    kwargs = {}
    if grid is None:
        in_specs = in_specs or [vmem] * len(operands)
        out_specs = [vmem] * len(out_shapes)
    else:
        kwargs["grid"] = grid
    return pl.pallas_call(
        kernel,
        out_shape=out_shapes,
        in_specs=in_specs,
        out_specs=out_specs,
        scratch_shapes=list(scratch),
        input_output_aliases=aliases or {},
        cost_estimate=pl.CostEstimate(flops=1, bytes_accessed=1, transcendentals=0),
        compiler_params=pltpu.CompilerParams(vmem_limit_bytes=vmem_bytes),
        **kwargs,
    )(*operands)


def f32(*shape):
    return jax.ShapeDtypeStruct(shape, F32)


def b16(*shape):
    return jax.ShapeDtypeStruct(shape, BF16)


def whole(shape):
    return pl.BlockSpec(shape, lambda *_: (0,) * len(shape))


def by_tokens(tokens, width):
    return pl.BlockSpec((tokens, width), lambda i: (i, 0))


def slot_weights(bits_ref, w_ref, bit, sections):
    chosen = w_ref[0, sections]
    for s in range(sections - 1):
        chosen = jnp.where(bits_ref[0, s] == bit, w_ref[0, 1 + s], chosen)
    return chosen


def put_left(out_ref, left, block):
    rows, rank = left.shape
    pieces = block // rank
    step = rows // pieces
    for p in range(pieces):
        out_ref[:step, p * rank : (p + 1) * rank] = left[p * step : (p + 1) * step]


def pack_kernel(bits_ref, w_ref, left_ref, right_ref, x_ref, g_ref, near_ref, far_ref, own_ref):
    _, slots, rows, block = w_ref.shape
    sections = slots - 1
    rank_rows = right_ref.shape[1]
    flat = far_ref.shape[0] - x_ref.shape[0]
    near_ref[:rows] = slot_weights(bits_ref, w_ref, 0, sections)
    near_ref[rows : rows + rank_rows] = right_ref[0]
    near_ref[rows + rank_rows :] = g_ref[...]
    put_left(far_ref.at[:flat], left_ref[0], block)
    far_ref[flat:] = x_ref[...]
    own_ref[:rows] = w_ref[0, 0]
    for b in range(1, sections):
        own_ref[b * rows : (b + 1) * rows] = slot_weights(bits_ref, w_ref, b, sections)
    at = sections * rows
    own_ref[at : at + rank_rows] = right_ref[0]
    put_left(own_ref.at[at + rank_rows :], left_ref[0], block)


def codes_of(x, g, far, near, low):
    lh, ll, rh, rl = low
    codes = nn(x, (lh[0], ll[0])) + nn(far, (lh[1], ll[1]))
    return codes, nt(g, (rh[0], rl[0])) + nt(near, (rh[1], rl[1]))


def sends_of(x, g, codes, code_grads, wide, low, ahead_ref, back_refs):
    wh, wl = wide
    lh, ll, rh, rl = low
    last = wh.shape[0] - 1
    ahead_ref[...] = nn(x, (wh[last], wl[last])) + nn(codes, (rh[1], rl[1]))
    for b in range(last):
        back = nt(g, (wh[b], wl[b]))
        if b == 0:
            back += nt(code_grads, (lh[1], ll[1]))
        back_refs[b][...] = back


def messages(x_ref, g_ref, far_ref, near_ref, wide, low, outs):
    x, g = split(x_ref[...]), split(g_ref[...])
    codes, code_grads = codes_of(x, g, split(far_ref[...]), split(near_ref[...]), low)
    outs[0][...] = codes
    outs[1][...] = code_grads
    sends_of(x, g, split(codes), split(code_grads), wide, low, outs[2], outs[3:])


def weights_kernel(sizes, *refs):
    sections, rows, rank_rows, rank, dp_count = sizes
    even_ref, odd_ref = refs[:2]
    early = refs[2:6] if sections == 2 else ()
    sh, sl, wh, wl, lh, ll, rh, rl, *outs = refs[2 + len(early) :]
    block = wh.shape[2]
    flat = rows * rank // block
    pieces = rows // flat
    me = lax.axis_index("dp")
    for k in range(dp_count):
        part = (odd_ref if k % 2 else even_ref).at[k // 2]
        owner = me ^ k
        at = 0

        def move(high_ref, low_ref, i, start, count, value):
            high, low = split(value)
            place = pl.ds(pl.multiple_of(start, 16), count)
            high_ref[i, place, :] = high
            low_ref[i, place, :] = low

        def move_wide(high_ref, low_ref, i, start, count):
            move(high_ref, low_ref, i, owner * count, count, part[start : start + count, :])
            return start + count

        def move_left(i, start):
            for p in range(pieces):
                value = part[start : start + flat, p * rank : (p + 1) * rank]
                move(lh, ll, i, owner * rows + p * flat, flat, value)
            return start + flat

        at = move_wide(sh, sl, 0, at, rows)
        for i in range(sections - 1):
            at = move_wide(wh, wl, i, at, rows)
        at = move_wide(rh, rl, 0, at, rank_rows)
        at = move_left(0, at)
        at = move_wide(wh, wl, sections - 1, at, rows)
        at = move_wide(rh, rl, 1, at, rank_rows)
        at = move_left(1, at)
    if early:
        messages(*early, (wh, wl), (lh, ll, rh, rl), outs)


def messages_kernel(x_ref, g_ref, far_ref, near_ref, wh, wl, lh, ll, rh, rl, *outs):
    messages(x_ref, g_ref, far_ref, near_ref, (wh, wl), (lh, ll, rh, rl), outs)


def codes_kernel(x_ref, g_ref, far_ref, near_ref, lh, ll, rh, rl, c_ref, cg_ref):
    parts = [split(r[...]) for r in (x_ref, g_ref, far_ref, near_ref)]
    c_ref[...], cg_ref[...] = codes_of(*parts, (lh, ll, rh, rl))


def sends_kernel(x_ref, g_ref, c_ref, cg_ref, wh, wl, lh, ll, rh, rl, *outs):
    parts = [split(r[...]) for r in (x_ref, g_ref, c_ref, cg_ref)]
    sends_of(*parts, (wh, wl), (lh, ll, rh, rl), outs[0], outs[1:])


def spread(dp_count, count, keep_refs, give_ref, put):
    me = lax.axis_index("dp")
    for k in range(dp_count):
        place = pl.ds(pl.multiple_of((me ^ k) * count, 8), count)
        put(give_ref.at[k // 2] if k % 2 else keep_refs[k // 2], place)


def self_kernel(sizes, scale, *refs):
    _, rows, _, _, dp_count = sizes
    x_ref, g_ref, *keep_refs, give_ref, dw = refs
    dw[...] = tn(split(x_ref[...]), split(g_ref[...])) * scale

    def put(out, place):
        out[...] = dw[place, :]

    spread(dp_count, rows, keep_refs, give_ref, put)


def grads_kernel(sizes, scale, *refs):
    sections, rows, rank_rows, rank, dp_count = sizes
    x_ref, g_ref, near_ref, c_ref, cg_ref, *rest = refs
    far_refs = rest[: sections - 1]
    half = dp_count // 2
    keep_refs = rest[sections - 1 : sections - 1 + half]
    give_ref = rest[sections - 1 + half]
    dw, dr, dl = rest[sections + half :]
    block = x_ref.shape[1]
    flat = rows * rank // block
    pieces = rows // flat
    at = [0]

    def spread_wide(source, count):
        def put(out, place):
            out[at[0] : at[0] + count, :] = source[place, :]

        spread(dp_count, count, keep_refs, give_ref, put)
        at[0] += count

    def spread_left(source):
        def put(out, place):
            value = source[place, :]
            for p in range(pieces):
                out[at[0] : at[0] + flat, p * rank : (p + 1) * rank] = value[
                    p * flat : (p + 1) * flat
                ]

        spread(dp_count, rows, keep_refs, give_ref, put)
        at[0] += flat

    x, g, near = split(x_ref[...]), split(g_ref[...]), split(near_ref[...])
    c, cg = split(c_ref[...]), split(cg_ref[...])
    far = [split(r[...]) for r in far_refs]
    dw[...] = tn(x, near) * scale
    spread_wide(dw, rows)
    dr[...] = tn(c, near) * scale
    spread_wide(dr, rank_rows)
    dl[...] = tn(far[0], cg) * scale
    spread_left(dl)
    for b in range(1, sections):
        dw[...] = tn(far[b - 1], g) * scale
        spread_wide(dw, rows)
    dr[...] = tn(c, g) * scale
    spread_wide(dr, rank_rows)
    dl[...] = tn(x, cg) * scale
    spread_left(dl)


def local_kernel(sections, *refs):
    x_ref, g_ref, near_ref, c_ref, cg_ref, *rest = refs
    far_refs = rest[: sections - 1]
    sh, sl, wh, wl, lh, ll, rh, rl, out_ref, grad_ref = rest[sections - 1 :]
    out = nn(split(x_ref[...]), (sh[0], sl[0])) + nn(split(c_ref[...]), (rh[0], rl[0]))
    for b in range(1, sections):
        out += nn(split(far_refs[b - 1][...]), (wh[b - 1], wl[b - 1]))
    out_ref[...] = out
    grad = nt(split(g_ref[...]), (sh[0], sl[0])) + nt(split(cg_ref[...]), (lh[0], ll[0]))
    grad_ref[...] = grad + nt(split(near_ref[...]), (wh[sections - 1], wl[sections - 1]))


def join_kernel(out0_ref, grad0_ref, ahead_ref, back_ref, out_ref, grad_ref):
    out_ref[...] = out0_ref[...] + ahead_ref[...]
    grad_ref[...] = grad0_ref[...] + back_ref[...]


def place_kernel(sizes, *refs):
    sections, rows, rank_rows, rank, _ = sizes
    bits_ref, self_ref, kept_ref, near_ref, far_ref, w_ref, left_ref, right_ref = refs
    block = kept_ref.shape[1]
    flat = rows * rank // block
    pieces = rows // flat
    w_ref[0, 0] = self_ref[...]
    for s in range(sections):
        chosen = near_ref[:rows]
        for b in range(1, sections):
            chosen = jnp.where(bits_ref[0, s] == b, kept_ref[(b - 1) * rows : b * rows], chosen)
        w_ref[0, 1 + s] = chosen
    at = (sections - 1) * rows
    right_ref[0] = kept_ref[at : at + rank_rows] + near_ref[rows:]
    at += rank_rows
    for p in range(pieces):
        columns = slice(p * rank, (p + 1) * rank)
        left_ref[0, p * flat : (p + 1) * flat, :] = (
            kept_ref[at : at + flat, columns] + far_ref[:, columns]
        )


def join(outputs, grad, parts, start):
    tokens, block = outputs.shape
    step = math.gcd(start, parts[0].shape[0])
    there = pl.BlockSpec((step, block), lambda i: (i + start // step, 0))
    here = by_tokens(step, block)
    return call(
        join_kernel,
        [f32(tokens, block)] * 2,
        [outputs, grad, *parts],
        grid=(parts[0].shape[0] // step,),
        in_specs=[there, there, here, here],
        out_specs=[there, there],
        aliases={0: 0, 1: 1},
    )


def on_device(inputs, partner_bits, block_weights, low_left, low_right, cotangent):
    tokens, block = inputs.shape
    sections = partner_bits.shape[1]
    dp_count = lax.axis_size("dp")
    half = dp_count // 2
    rows, rank = low_left.shape[1:]
    rank_rows = low_right.shape[1]
    all_rank = rank_rows * dp_count
    flat = rows * rank // block
    sizes = (sections, rows, rank_rows, rank, dp_count)
    early = tokens * 3 // 128 * 16
    late = tokens - early
    lent_rows = rows + rank_rows
    own_rows = sections * rows + rank_rows + flat
    sum_rows = own_rows + lent_rows + flat - rows
    smem = pl.BlockSpec(memory_space=pltpu.SMEM)
    vmem = pl.BlockSpec(memory_space=pltpu.VMEM)
    usual = partner_bits[0, 0] >= 0

    by_slot = jnp.transpose(block_weights, (0, 2, 1, 3))
    pack_shapes = [(lent_rows + early, block), (flat + early, block), (own_rows, block)]
    out_near, out_far, own = call(
        pack_kernel,
        [f32(*s) for s in pack_shapes],
        [partner_bits, by_slot, low_left, low_right, inputs, cotangent],
        grid=(1,),
        in_specs=[
            smem, whole(by_slot.shape), whole(low_left.shape), whole(low_right.shape),
            whole((early, block)), whole((early, block)),
        ],
        out_specs=[whole(s) for s in pack_shapes],
        vmem_bytes=PACK_VMEM_BYTES,
    )
    got_near = across(out_near, "feat", 1)
    got_far = across(out_far, "feat", 2)
    own = [own] + [across(own, "dp", k) for k in range(2, dp_count, 2)]
    late_x, late_g, got_near, got_far, own = lax.optimization_barrier(
        (inputs[early:], cotangent[early:], got_near, got_far, own)
    )
    late_far = across(late_x, "feat", 2)
    late_near = across(late_g, "feat", 1)
    early_far, early_near = got_far[flat:], got_near[lent_rows:]

    s_shape = (1, block, block)
    w_shape = (sections, block, block)
    l_shape = (2, block, rank)
    r_shape = (2, all_rank, block)
    shapes = [s_shape, s_shape, w_shape, w_shape, l_shape, l_shape, r_shape, r_shape]

    def message_shapes(count):
        return [(count, rank)] * 2 + [(count, block)] * sections

    folds = sections == 2
    scale = 1.0 / math.sqrt(tokens * dp_count)
    made = [b16(*s) for s in shapes]
    if folds:
        made += [f32(*s) for s in message_shapes(early)]

    lent = jnp.concatenate([got_near[:lent_rows], got_far[:flat]])
    lent = [lent] + [across(lent, "dp", k) for k in range(2, dp_count, 2)]

    def prepare(own, lent, *early_parts):
        even = jnp.stack([jnp.concatenate(pair) for pair in zip(own, lent)])
        odd = across(even, "dp", 1)
        *keep, give = call(
            functools.partial(self_kernel, sizes, scale),
            [f32(rows, block)] * half + [f32(half, rows, block)],
            early_parts[:2],
            scratch=[pltpu.VMEM((block, block), F32)],
        )
        got = across(give, "dp", 1)
        got, odd = lax.optimization_barrier((got, odd))
        self_grads = keep[0] + got[0]
        for m in range(1, half):
            self_grads = self_grads + across(keep[m] + got[m], "dp", 2 * m)
        operands = [even, odd, *early_parts] if folds else [even, odd]
        return self_grads, *(
            call(
                functools.partial(weights_kernel, sizes),
                made,
                operands,
                grid=(1,),
                in_specs=[whole(even.shape)] * 2 + [whole((early, block))] * (len(operands) - 2),
                out_specs=[whole(s.shape) for s in made],
            )
        )

    def empty(*_):
        return tuple(jnp.zeros(s.shape, s.dtype) for s in [f32(rows, block)] + made)

    self_grads, *weights = lax.cond(
        usual, prepare, empty,
        own, lent, inputs, cotangent, early_far, early_near,
    )
    weights, sent = weights[:8], weights[8:]
    low = weights[4:]
    step = tokens // 2
    wide, thin = by_tokens(step, block), by_tokens(step, rank)
    weight_specs = [whole(s) for s in shapes]
    if folds:
        wide_late, thin_late = by_tokens(late, block), by_tokens(late, rank)
        late_sent = call(
            messages_kernel,
            [f32(*s) for s in message_shapes(late)],
            [late_x, late_g, late_far, late_near, *weights[2:]],
            grid=(1,),
            in_specs=[wide_late] * 4 + weight_specs[2:],
            out_specs=[thin_late] * 2 + [wide_late] * sections,
        )
        first = [across(sent[2], "feat", 1), across(sent[3], "feat", 2)]
        codes = jnp.concatenate([sent[0], late_sent[0]])
        code_grads = jnp.concatenate([sent[1], late_sent[1]])
    far = [jnp.concatenate([early_far, late_far])]
    near = jnp.concatenate([early_near, late_near])
    far += [across(inputs, "feat", 1 << b) for b in range(2, sections)]
    grid = (tokens // step,)
    if not folds:
        codes, code_grads = call(
            codes_kernel,
            [f32(tokens, rank)] * 2,
            [inputs, cotangent, far[0], near, *low],
            grid=grid,
            in_specs=[wide] * 4 + weight_specs[4:],
            out_specs=[thin, thin],
        )
        for b in range(2, sections):
            codes = codes + across(codes, "feat", 1 << b)
            code_grads = code_grads + across(code_grads, "feat", 1 << b)
        ahead, *back = call(
            sends_kernel,
            [f32(tokens, block)] * sections,
            [inputs, cotangent, codes, code_grads, *weights[2:]],
            grid=grid,
            in_specs=[wide, wide, thin, thin, *weight_specs[2:]],
            out_specs=[wide] * sections,
        )
        back = [across(back[b - 1], "feat", 1 << b) for b in range(1, sections)]
        ahead = across(ahead, "feat", 1)

    def reduce_pair(inputs, cotangent, near, codes, code_grads, *far):
        *keep, give = call(
            functools.partial(grads_kernel, sizes, scale),
            [f32(sum_rows, block)] * half + [f32(half, sum_rows, block)],
            [inputs, cotangent, near, codes, code_grads, *far],
            scratch=[
                pltpu.VMEM((block, block), F32),
                pltpu.VMEM((all_rank, block), F32),
                pltpu.VMEM((block, rank), F32),
            ],
        )
        got = across(give, "dp", 1)
        return tuple(keep[m] + got[m] for m in range(half))

    def no_pair(*_):
        return (jnp.zeros((sum_rows, block), F32),) * half

    summed = lax.cond(usual, reduce_pair, no_pair, inputs, cotangent, near, codes, code_grads, *far)
    if folds:
        first, rest, summed = lax.optimization_barrier((first, late_sent[2:], summed))
        rest = [across(rest[0], "feat", 1), across(rest[1], "feat", 2)]

    def finish(summed, inputs, cotangent, near, codes, code_grads, far, weights):
        total = summed[0]
        for m in range(1, half):
            total = total + across(summed[m], "dp", 2 * m)
        out, grad = call(
            functools.partial(local_kernel, sections),
            [f32(tokens, block)] * 2,
            [inputs, cotangent, near, codes, code_grads, *far, *weights],
            grid=grid,
            in_specs=[wide] * 3 + [thin] * 2 + [wide] * (sections - 1) + weight_specs,
            out_specs=[wide, wide],
        )
        at = lent_rows + flat
        return out, grad, total[:lent_rows], total[lent_rows:at], total[at:]

    def nothing(*_):
        wide_zero = jnp.zeros((tokens, block), F32)
        return (
            wide_zero, wide_zero, jnp.zeros((lent_rows, block), F32),
            jnp.zeros((flat, block), F32), jnp.zeros((sum_rows - lent_rows - flat, block), F32),
        )

    outputs, grad, near_back, far_back, kept = lax.cond(
        usual, finish, nothing,
        summed, inputs, cotangent, near, codes, code_grads, far, weights,
    )
    if folds:
        for start, parts in ((0, first), (early, rest)):
            outputs, grad = join(outputs, grad, parts, start)
    else:
        outputs = outputs + ahead
        for part in back:
            grad = grad + part
    near_back = across(near_back, "feat", 1)
    far_back = across(far_back, "feat", 2)
    outputs, grad, kept = lax.optimization_barrier((outputs, grad, kept))
    block_grads, left_grads, right_grads = call(
        functools.partial(place_kernel, sizes),
        [f32(*by_slot.shape), f32(*low_left.shape), f32(*low_right.shape)],
        [partner_bits, self_grads, kept, near_back, far_back],
        in_specs=[smem] + [vmem] * 4,
    )
    block_grads = jnp.transpose(block_grads, (0, 2, 1, 3))
    return (outputs, grad, block_grads, left_grads, right_grads)


def solution(mesh):
    in_specs = (
        P("dp", "feat"),
        P("feat", None),
        P("feat", "dp", None, None),
        P("feat", "dp", None),
        P("feat", "dp", None),
        P("dp", "feat"),
    )
    out_specs = (
        P("dp", "feat"),
        P("dp", "feat"),
        P("feat", "dp", None, None),
        P("feat", "dp", None),
        P("feat", "dp", None),
    )
    return jax.shard_map(
        on_device, mesh=mesh, in_specs=in_specs, out_specs=out_specs, check_vma=False
    )
```

```python
import functools
import math

import jax
import jax.numpy as jnp
from jax import lax
from jax.experimental import pallas as pl
from jax.experimental.pallas import tpu as pltpu
from jax.sharding import PartitionSpec as P

F32 = jnp.float32
BF16 = jnp.bfloat16
EARLY = 80
VMEM_BYTES = 20 * 1024 * 1024
JOIN_VMEM_BYTES = 8 * 1024 * 1024
PACK_VMEM_BYTES = 60 * 1024 * 1024


def across(block, axis, apart):
    count = lax.axis_size(axis)
    return lax.ppermute(block, axis, [(i, i ^ apart) for i in range(count)])


def scatter_rows(blocks, beside):
    bits = len(blocks).bit_length() - 1
    if not bits:
        return blocks[0], beside
    rows = blocks[0].shape[0]
    cuts = [rows * g // bits // 8 * 8 for g in range(bits)] + [rows]
    groups = [
        {m: block[cuts[g] : cuts[g + 1]] for m, block in enumerate(blocks)} for g in range(bits)
    ]
    for step in range(bits):
        turn = [(g + step) % bits for g in range(bits)]
        sent = [[m for m in group if m >> bit & 1] for group, bit in zip(groups, turn)]
        stacks = [jnp.stack([group[m] for m in ms]) for group, ms in zip(groups, sent)]
        stacks = lax.optimization_barrier(stacks)
        got = [across(stack, "dp", 2 << bit) for stack, bit in zip(stacks, turn)]
        got, beside = lax.optimization_barrier((got, beside))
        groups = [
            {m ^ 1 << bit: group[m ^ 1 << bit] + part[i] for i, m in enumerate(ms)}
            for group, ms, part, bit in zip(groups, sent, got, turn)
        ]
    return jnp.concatenate([group[0] for group in groups]), beside


def gather_rows(part, count):
    bits = (count // 2).bit_length() - 1
    if not bits:
        return [part]
    rows = part.shape[0]
    cuts = [rows * g // bits // 8 * 8 for g in range(bits)] + [rows]
    groups = [{0: part[cuts[g] : cuts[g + 1]]} for g in range(bits)]
    for step in range(bits):
        turn = [(g + step) % bits for g in range(bits)]
        stacks = [jnp.stack([group[m] for m in sorted(group)]) for group in groups]
        got = [across(stack, "dp", 2 << bit) for stack, bit in zip(stacks, turn)]
        got = lax.optimization_barrier(got)
        groups = [
            {**group, **{m ^ 1 << bit: more[i] for i, m in enumerate(sorted(group))}}
            for group, more, bit in zip(groups, got, turn)
        ]
    return [jnp.concatenate([group[m] for group in groups]) for m in range(count // 2)]


def split(value):
    high = value.astype(BF16)
    return high, (value - high.astype(F32)).astype(BF16)


def dot3(left, right, over):
    def one(a, b):
        return lax.dot_general(
            a, b, ((over[:1], over[1:]), ((), ())), preferred_element_type=F32
        )

    return one(left[0], right[0]) + (one(left[0], right[1]) + one(left[1], right[0]))


def nn(left, right):
    return dot3(left, right, (1, 0))


def nt(left, right):
    return dot3(left, right, (1, 1))


def tn(left, right):
    return dot3(left, right, (0, 0))


def call(
    kernel, out_shapes, operands, grid=None, in_specs=None, out_specs=None, scratch=(),
    vmem_bytes=VMEM_BYTES,
):
    vmem = pl.BlockSpec(memory_space=pltpu.VMEM)
    kwargs = {}
    if grid is None:
        in_specs = in_specs or [vmem] * len(operands)
        out_specs = [vmem] * len(out_shapes)
    else:
        kwargs["grid"] = grid
    return pl.pallas_call(
        kernel,
        out_shape=out_shapes,
        in_specs=in_specs,
        out_specs=out_specs,
        scratch_shapes=list(scratch),
        cost_estimate=pl.CostEstimate(flops=1, bytes_accessed=1, transcendentals=0),
        compiler_params=pltpu.CompilerParams(vmem_limit_bytes=vmem_bytes),
        **kwargs,
    )(*operands)


def f32(*shape):
    return jax.ShapeDtypeStruct(shape, F32)


def b16(*shape):
    return jax.ShapeDtypeStruct(shape, BF16)


def whole(shape):
    return pl.BlockSpec(shape, lambda *_: (0,) * len(shape))


def by_tokens(tokens, width):
    return pl.BlockSpec((tokens, width), lambda i: (i, 0))


def slot_weights(bits_ref, w_ref, bit, sections):
    chosen = w_ref[0, sections]
    for s in range(sections - 1):
        chosen = jnp.where(bits_ref[0, s] == bit, w_ref[0, 1 + s], chosen)
    return chosen


def put_left(out_ref, left, block):
    rows, rank = left.shape
    pieces = block // rank
    step = rows // pieces
    for p in range(pieces):
        out_ref[:step, p * rank : (p + 1) * rank] = left[p * step : (p + 1) * step]


def pack_kernel(bits_ref, w_ref, left_ref, right_ref, x_ref, g_ref, near_ref, far_ref, own_ref):
    _, slots, rows, block = w_ref.shape
    sections = slots - 1
    rank_rows = right_ref.shape[1]
    flat = far_ref.shape[0] - x_ref.shape[0]
    near_ref[:rows] = slot_weights(bits_ref, w_ref, 0, sections)
    near_ref[rows : rows + rank_rows] = right_ref[0]
    near_ref[rows + rank_rows :] = g_ref[...]
    put_left(far_ref.at[:flat], left_ref[0], block)
    far_ref[flat:] = x_ref[...]
    own_ref[:rows] = w_ref[0, 0]
    for b in range(1, sections):
        own_ref[b * rows : (b + 1) * rows] = slot_weights(bits_ref, w_ref, b, sections)
    at = sections * rows
    own_ref[at : at + rank_rows] = right_ref[0]
    put_left(own_ref.at[at + rank_rows :], left_ref[0], block)


def codes_of(x, g, far, near, low):
    lh, ll, rh, rl = low
    codes = nn(x, (lh[0], ll[0])) + nn(far, (lh[1], ll[1]))
    return codes, nt(g, (rh[0], rl[0])) + nt(near, (rh[1], rl[1]))


def put_rows(refs, value):
    at = 0
    for ref in refs:
        ref[...] = value[at : at + ref.shape[0]]
        at += ref.shape[0]


def sends_of(x, g, codes, code_grads, wide, low, outs):
    wh, wl = wide
    lh, ll, rh, rl = low
    last = wh.shape[0] - 1
    cuts = len(outs) // (last + 1)
    put_rows(outs[:cuts], nn(x, (wh[last], wl[last])) + nn(codes, (rh[1], rl[1])))
    for b in range(last):
        back = nt(g, (wh[b], wl[b]))
        if b == 0:
            back += nt(code_grads, (lh[1], ll[1]))
        put_rows(outs[(b + 1) * cuts : (b + 2) * cuts], back)


def messages(x_ref, g_ref, far_ref, near_ref, wide, low, outs):
    x, g = split(x_ref[...]), split(g_ref[...])
    codes, code_grads = codes_of(x, g, split(far_ref[...]), split(near_ref[...]), low)
    outs[0][...] = codes
    outs[1][...] = code_grads
    sends_of(x, g, split(codes), split(code_grads), wide, low, outs[2:])


def weights_kernel(sizes, *refs):
    sections, rows, rank_rows, rank, dp_count = sizes
    even_ref, odd_ref = refs[:2]
    early = refs[2:6] if sections == 2 else ()
    sh, sl, wh, wl, lh, ll, rh, rl, *outs = refs[2 + len(early) :]
    block = wh.shape[2]
    flat = rows * rank // block
    pieces = rows // flat
    me = lax.axis_index("dp")
    for k in range(dp_count):
        part = (odd_ref if k % 2 else even_ref).at[k // 2]
        owner = me ^ k
        at = 0

        def move(high_ref, low_ref, i, start, count, value):
            high, low = split(value)
            place = pl.ds(pl.multiple_of(start, 16), count)
            high_ref[i, place, :] = high
            low_ref[i, place, :] = low

        def move_wide(high_ref, low_ref, i, start, count):
            move(high_ref, low_ref, i, owner * count, count, part[start : start + count, :])
            return start + count

        def move_left(i, start):
            for p in range(pieces):
                value = part[start : start + flat, p * rank : (p + 1) * rank]
                move(lh, ll, i, owner * rows + p * flat, flat, value)
            return start + flat

        at = move_wide(sh, sl, 0, at, rows)
        for i in range(sections - 1):
            at = move_wide(wh, wl, i, at, rows)
        at = move_wide(rh, rl, 0, at, rank_rows)
        at = move_left(0, at)
        at = move_wide(wh, wl, sections - 1, at, rows)
        at = move_wide(rh, rl, 1, at, rank_rows)
        at = move_left(1, at)
    if early:
        messages(*early, (wh, wl), (lh, ll, rh, rl), outs)


def messages_kernel(x_ref, g_ref, far_ref, near_ref, wh, wl, lh, ll, rh, rl, *outs):
    messages(x_ref, g_ref, far_ref, near_ref, (wh, wl), (lh, ll, rh, rl), outs)


def codes_kernel(x_ref, g_ref, far_ref, near_ref, lh, ll, rh, rl, c_ref, cg_ref):
    parts = [split(r[...]) for r in (x_ref, g_ref, far_ref, near_ref)]
    c_ref[...], cg_ref[...] = codes_of(*parts, (lh, ll, rh, rl))


def sends_kernel(x_ref, g_ref, c_ref, cg_ref, wh, wl, lh, ll, rh, rl, *outs):
    parts = [split(r[...]) for r in (x_ref, g_ref, c_ref, cg_ref)]
    sends_of(*parts, (wh, wl), (lh, ll, rh, rl), outs)


def spread(dp_count, count, keep_refs, give_ref, put):
    me = lax.axis_index("dp")
    for k in range(dp_count):
        place = pl.ds(pl.multiple_of((me ^ k) * count, 8), count)
        put(give_ref.at[k // 2] if k % 2 else keep_refs[k // 2], place)


def self_kernel(sizes, scale, *refs):
    _, rows, _, _, dp_count = sizes
    x_ref, g_ref, *keep_refs, give_ref, dw = refs
    dw[...] = tn(split(x_ref[...]), split(g_ref[...])) * scale

    def put(out, place):
        out[...] = dw[place, :]

    spread(dp_count, rows, keep_refs, give_ref, put)


def cat(refs):
    values = [r[...] for r in refs]
    return values[0] if len(values) == 1 else jnp.concatenate(values, axis=0)


def take_pieces(refs, counts):
    groups, at = [], 0
    for count in counts:
        groups.append(cat(refs[at : at + count]))
        at += count
    return [split(group) for group in groups], refs[at:]


def grads_kernel(sizes, scale, counts, *refs):
    sections, rows, rank_rows, rank, dp_count = sizes
    (x, g, near, c, cg, *far), rest = take_pieces(refs, counts)
    half = dp_count // 2
    keep_refs = rest[:half]
    give_ref, dw, dr, dl = rest[half:]
    block = dw.shape[1]
    flat = rows * rank // block
    pieces = rows // flat
    at = [0]

    def spread_wide(source, count):
        def put(out, place):
            out[at[0] : at[0] + count, :] = source[place, :]

        spread(dp_count, count, keep_refs, give_ref, put)
        at[0] += count

    def spread_left(source):
        def put(out, place):
            value = source[place, :]
            for p in range(pieces):
                out[at[0] : at[0] + flat, p * rank : (p + 1) * rank] = value[
                    p * flat : (p + 1) * flat
                ]

        spread(dp_count, rows, keep_refs, give_ref, put)
        at[0] += flat

    dw[...] = tn(x, near) * scale
    spread_wide(dw, rows)
    dr[...] = tn(c, near) * scale
    spread_wide(dr, rank_rows)
    dl[...] = tn(far[0], cg) * scale
    spread_left(dl)
    for b in range(1, sections):
        dw[...] = tn(far[b - 1], g) * scale
        spread_wide(dw, rows)
    dr[...] = tn(c, g) * scale
    spread_wide(dr, rank_rows)
    dl[...] = tn(x, cg) * scale
    spread_left(dl)


def local_kernel(counts, *refs):
    (x, g, near, c, cg, *far), rest = take_pieces(refs, counts)
    sh, sl, wh, wl, lh, ll, rh, rl, *first, out_ref, grad_ref = rest
    last = wh.shape[0] - 1
    out = nn(x, (sh[0], sl[0])) + nn(c, (rh[0], rl[0]))
    for b in range(last):
        out += nn(far[b], (wh[b], wl[b]))
    out_ref[...] = out
    grad = nt(g, (sh[0], sl[0])) + nt(cg, (lh[0], ll[0]))
    grad_ref[...] = grad + nt(near, (wh[last], wl[last]))
    if first:
        ahead_ref, back_ref = first
        count = ahead_ref.shape[0]
        out_ref[:count] += ahead_ref[...]
        grad_ref[:count] += back_ref[...]


def join_kernel(whole_ref, late_ref, out_ref):
    early = whole_ref.shape[0] - late_ref.shape[0]
    out_ref[:early] = whole_ref[:early]
    out_ref[early:] = whole_ref[early:] + late_ref[...]


def place_kernel(sizes, *refs):
    sections, rows, rank_rows, rank, _ = sizes
    bits_ref, self_ref, kept_ref, near_ref, far_ref, w_ref, left_ref, right_ref = refs
    block = kept_ref.shape[1]
    flat = rows * rank // block
    pieces = rows // flat
    w_ref[0, 0] = self_ref[...]
    for s in range(sections):
        chosen = near_ref[:rows]
        for b in range(1, sections):
            chosen = jnp.where(bits_ref[0, s] == b, kept_ref[(b - 1) * rows : b * rows], chosen)
        w_ref[0, 1 + s] = chosen
    at = (sections - 1) * rows
    right_ref[0] = kept_ref[at : at + rank_rows] + near_ref[rows:]
    at += rank_rows
    for p in range(pieces):
        columns = slice(p * rank, (p + 1) * rank)
        left_ref[0, p * flat : (p + 1) * flat, :] = (
            kept_ref[at : at + flat, columns] + far_ref[:, columns]
        )


def on_device(inputs, partner_bits, block_weights, low_left, low_right, cotangent):
    tokens, block = inputs.shape
    sections = partner_bits.shape[1]
    dp_count = lax.axis_size("dp")
    half = dp_count // 2
    rows, rank = low_left.shape[1:]
    rank_rows = low_right.shape[1]
    all_rank = rank_rows * dp_count
    flat = rows * rank // block
    sizes = (sections, rows, rank_rows, rank, dp_count)
    early = tokens * EARLY // 512 // 16 * 16
    late = tokens - early
    lent_rows = rows + rank_rows
    own_rows = sections * rows + rank_rows + flat
    sum_rows = own_rows + lent_rows + flat - rows
    smem = pl.BlockSpec(memory_space=pltpu.SMEM)
    vmem = pl.BlockSpec(memory_space=pltpu.VMEM)
    usual = partner_bits[0, 0] >= 0
    folds = sections == 2
    scale = 1.0 / math.sqrt(tokens * dp_count)

    by_slot = jnp.transpose(block_weights, (0, 2, 1, 3))
    pack_shapes = [(lent_rows + early, block), (flat + early, block), (own_rows, block)]
    out_near, out_far, own = call(
        pack_kernel,
        [f32(*s) for s in pack_shapes],
        [partner_bits, by_slot, low_left, low_right, inputs, cotangent],
        grid=(1,),
        in_specs=[
            smem, whole(by_slot.shape), whole(low_left.shape), whole(low_right.shape),
            whole((early, block)), whole((early, block)),
        ],
        out_specs=[whole(s) for s in pack_shapes],
        vmem_bytes=PACK_VMEM_BYTES,
    )
    got_near = across(out_near, "feat", 1)
    got_far = across(out_far, "feat", 2)
    own = [own] + [across(own, "dp", k) for k in range(2, dp_count, 2)]
    late_x, got_far = lax.optimization_barrier((inputs[early:], got_far))
    late_far = across(late_x, "feat", 2)
    late_g, got_near = lax.optimization_barrier((cotangent[early:], got_near))
    late_near = across(late_g, "feat", 1)
    early_far, early_near = got_far[flat:], got_near[lent_rows:]
    lent = jnp.concatenate([got_near[:lent_rows], got_far[:flat]])
    lent, own = lax.optimization_barrier((lent, own))
    lent = gather_rows(lent, dp_count)
    *self_keep, self_give = call(
        functools.partial(self_kernel, sizes, scale),
        [f32(rows, block)] * half + [f32(half, rows, block)],
        [inputs, cotangent],
        scratch=[pltpu.VMEM((block, block), F32)],
    )

    s_shape = (1, block, block)
    w_shape = (sections, block, block)
    l_shape = (2, block, rank)
    r_shape = (2, all_rank, block)
    shapes = [s_shape, s_shape, w_shape, w_shape, l_shape, l_shape, r_shape, r_shape]

    def message_shapes(*cuts):
        sends = [(cut, block) for cut in cuts] * sections
        return [(sum(cuts), rank)] * 2 + sends

    made = [b16(*s) for s in shapes]
    if folds:
        made += [f32(*s) for s in message_shapes(early)]

    def prepare(own, lent, keep, give, *early_parts):
        even = jnp.stack([jnp.concatenate(pair) for pair in zip(own, lent)])
        odd = across(even, "dp", 1)
        got = across(give, "dp", 1)
        got, odd = lax.optimization_barrier((got, odd))
        self_grads = keep[0] + got[0]
        for m in range(1, half):
            self_grads = self_grads + across(keep[m] + got[m], "dp", 2 * m)
        operands = [even, odd, *early_parts] if folds else [even, odd]
        return self_grads, *(
            call(
                functools.partial(weights_kernel, sizes),
                made,
                operands,
                grid=(1,),
                in_specs=[whole(even.shape)] * 2 + [whole((early, block))] * (len(operands) - 2),
                out_specs=[whole(s.shape) for s in made],
            )
        )

    def empty(*_):
        return tuple(jnp.zeros(s.shape, s.dtype) for s in [f32(rows, block)] + made)

    self_grads, *weights = lax.cond(
        usual, prepare, empty,
        own, lent, self_keep, self_give, inputs, cotangent, early_far, early_near,
    )
    weights, sent = weights[:8], weights[8:]
    weight_specs = [whole(s) for s in shapes]
    near = [early_near, late_near]
    far = [[early_far, late_far]]
    if folds:
        late_shapes = message_shapes(late)
        late_sent = call(
            messages_kernel,
            [f32(*s) for s in late_shapes],
            [late_x, late_g, late_far, late_near, *weights[2:]],
            grid=(1,),
            in_specs=[whole((late, block))] * 4 + weight_specs[2:],
            out_specs=[whole(s) for s in late_shapes],
        )
        first = [across(part, "feat", 1 << b) for b, part in enumerate(sent[2:])]
        rest = list(late_sent[2:])
        rest[0], first[1] = lax.optimization_barrier((rest[0], first[1]))
        rest[1], first[0] = lax.optimization_barrier((rest[1], first[0]))
        first, late_sent = lax.optimization_barrier((first, late_sent))
        rest = [across(part, "feat", 1 << b) for b, part in enumerate(rest)]
        codes, code_grads = ([sent[i], late_sent[i]] for i in range(2))
    else:
        far += [[across(inputs, "feat", 1 << b)] for b in range(2, sections)]
        step = tokens // 2
        wide, thin = by_tokens(step, block), by_tokens(step, rank)
        codes, code_grads = call(
            codes_kernel,
            [f32(tokens, rank)] * 2,
            [inputs, cotangent, jnp.concatenate(far[0]), jnp.concatenate(near), *weights[4:]],
            grid=(2,),
            in_specs=[wide] * 4 + weight_specs[4:],
            out_specs=[thin, thin],
        )
        for b in range(2, sections):
            codes = codes + across(codes, "feat", 1 << b)
            code_grads = code_grads + across(code_grads, "feat", 1 << b)
        messages = call(
            sends_kernel,
            [f32(tokens, block)] * sections,
            [inputs, cotangent, codes, code_grads, *weights[2:]],
            grid=(2,),
            in_specs=[wide, wide, thin, thin, *weight_specs[2:]],
            out_specs=[wide] * sections,
        )
        messages = [across(part, "feat", 1 << b) for b, part in enumerate(messages)]
        codes, code_grads = [codes], [code_grads]

    groups = [[inputs], [cotangent], near, codes, code_grads, *far]
    counts = [len(group) for group in groups]

    def finish(groups, weights, first):
        *keep, give = call(
            functools.partial(grads_kernel, sizes, scale, counts),
            [f32(sum_rows, block)] * half + [f32(half, sum_rows, block)],
            [part for group in groups for part in group],
            scratch=[
                pltpu.VMEM((block, block), F32),
                pltpu.VMEM((all_rank, block), F32),
                pltpu.VMEM((block, rank), F32),
            ],
        )
        groups, give = lax.optimization_barrier((groups, give))
        got = across(give, "dp", 1)
        beside = call(
            functools.partial(local_kernel, counts),
            [f32(tokens, block)] * 2,
            [part for group in groups for part in group] + weights + first,
        )
        total, (out, grad) = scatter_rows([keep[m] + got[m] for m in range(half)], beside)
        at = lent_rows + flat
        return out, grad, total[:lent_rows], total[lent_rows:at], total[at:]

    def nothing(*_):
        shapes = [(tokens, block)] * 2 + [(n, block) for n in (lent_rows, flat, own_rows - rows)]
        return tuple(jnp.zeros(shape, F32) for shape in shapes)

    outputs, grad, near_back, far_back, kept = lax.cond(
        usual, finish, nothing, groups, weights, first if folds else []
    )
    near_back = across(near_back, "feat", 1)
    far_back = across(far_back, "feat", 2)
    if folds:
        outputs, grad = (
            call(join_kernel, [f32(tokens, block)], parts, vmem_bytes=JOIN_VMEM_BYTES)[0]
            for parts in zip((outputs, grad), rest)
        )
    else:
        outputs = outputs + messages[0]
        for part in messages[1:]:
            grad = grad + part
    outputs, grad, kept = lax.optimization_barrier((outputs, grad, kept))
    block_grads, left_grads, right_grads = call(
        functools.partial(place_kernel, sizes),
        [f32(*by_slot.shape), f32(*low_left.shape), f32(*low_right.shape)],
        [partner_bits, self_grads, kept, near_back, far_back],
        in_specs=[smem] + [vmem] * 4,
    )
    block_grads = jnp.transpose(block_grads, (0, 2, 1, 3))
    return (outputs, grad, block_grads, left_grads, right_grads)


def solution(mesh):
    in_specs = (
        P("dp", "feat"),
        P("feat", None),
        P("feat", "dp", None, None),
        P("feat", "dp", None),
        P("feat", "dp", None),
        P("dp", "feat"),
    )
    out_specs = (
        P("dp", "feat"),
        P("dp", "feat"),
        P("feat", "dp", None, None),
        P("feat", "dp", None),
        P("feat", "dp", None),
    )
    return jax.shard_map(
        on_device, mesh=mesh, in_specs=in_specs, out_specs=out_specs, check_vma=False
    )
```

```python
import functools
import math

import jax
import jax.numpy as jnp
from jax import lax
from jax.experimental import pallas as pl
from jax.experimental.pallas import tpu as pltpu
from jax.sharding import PartitionSpec as P

F32 = jnp.float32
BF16 = jnp.bfloat16
EARLY = 48
VMEM_BYTES = 20 * 1024 * 1024
JOIN_VMEM_BYTES = 8 * 1024 * 1024
PACK_VMEM_BYTES = 60 * 1024 * 1024


def across(block, axis, apart):
    count = lax.axis_size(axis)
    return lax.ppermute(block, axis, [(i, i ^ apart) for i in range(count)])


def scatter_rows(blocks, beside):
    bits = len(blocks).bit_length() - 1
    if not bits:
        return blocks[0], beside
    rows = blocks[0].shape[0]
    cuts = [rows * g // bits // 8 * 8 for g in range(bits)] + [rows]
    groups = [
        {m: block[cuts[g] : cuts[g + 1]] for m, block in enumerate(blocks)} for g in range(bits)
    ]
    for step in range(bits):
        turn = [(g + step) % bits for g in range(bits)]
        sent = [[m for m in group if m >> bit & 1] for group, bit in zip(groups, turn)]
        stacks = [jnp.stack([group[m] for m in ms]) for group, ms in zip(groups, sent)]
        stacks = lax.optimization_barrier(stacks)
        got = [across(stack, "dp", 2 << bit) for stack, bit in zip(stacks, turn)]
        got, beside = lax.optimization_barrier((got, beside))
        groups = [
            {m ^ 1 << bit: group[m ^ 1 << bit] + part[i] for i, m in enumerate(ms)}
            for group, ms, part, bit in zip(groups, sent, got, turn)
        ]
    return jnp.concatenate([group[0] for group in groups]), beside


def gather_rows(part, count):
    bits = (count // 2).bit_length() - 1
    if not bits:
        return [part]
    rows = part.shape[0]
    cuts = [rows * g // bits // 8 * 8 for g in range(bits)] + [rows]
    groups = [{0: part[cuts[g] : cuts[g + 1]]} for g in range(bits)]
    for step in range(bits):
        turn = [(g + step) % bits for g in range(bits)]
        stacks = [jnp.stack([group[m] for m in sorted(group)]) for group in groups]
        got = [across(stack, "dp", 2 << bit) for stack, bit in zip(stacks, turn)]
        got = lax.optimization_barrier(got)
        groups = [
            {**group, **{m ^ 1 << bit: more[i] for i, m in enumerate(sorted(group))}}
            for group, more, bit in zip(groups, got, turn)
        ]
    return [jnp.concatenate([group[m] for group in groups]) for m in range(count // 2)]


def split(value):
    high = value.astype(BF16)
    return high, (value - high.astype(F32)).astype(BF16)


def dot3(left, right, over):
    def one(a, b):
        return lax.dot_general(
            a, b, ((over[:1], over[1:]), ((), ())), preferred_element_type=F32
        )

    return one(left[0], right[0]) + (one(left[0], right[1]) + one(left[1], right[0]))


def nn(left, right):
    return dot3(left, right, (1, 0))


def nt(left, right):
    return dot3(left, right, (1, 1))


def tn(left, right):
    return dot3(left, right, (0, 0))


def call(
    kernel, out_shapes, operands, grid=None, in_specs=None, out_specs=None, scratch=(),
    vmem_bytes=VMEM_BYTES,
):
    vmem = pl.BlockSpec(memory_space=pltpu.VMEM)
    kwargs = {}
    if grid is None:
        in_specs = in_specs or [vmem] * len(operands)
        out_specs = [vmem] * len(out_shapes)
    else:
        kwargs["grid"] = grid
    return pl.pallas_call(
        kernel,
        out_shape=out_shapes,
        in_specs=in_specs,
        out_specs=out_specs,
        scratch_shapes=list(scratch),
        cost_estimate=pl.CostEstimate(flops=1, bytes_accessed=1, transcendentals=0),
        compiler_params=pltpu.CompilerParams(vmem_limit_bytes=vmem_bytes),
        **kwargs,
    )(*operands)


def f32(*shape):
    return jax.ShapeDtypeStruct(shape, F32)


def b16(*shape):
    return jax.ShapeDtypeStruct(shape, BF16)


def whole(shape):
    return pl.BlockSpec(shape, lambda *_: (0,) * len(shape))


def by_tokens(tokens, width):
    return pl.BlockSpec((tokens, width), lambda i: (i, 0))


def slot_weights(bits_ref, w_ref, bit, sections):
    chosen = w_ref[0, sections]
    for s in range(sections - 1):
        chosen = jnp.where(bits_ref[0, s] == bit, w_ref[0, 1 + s], chosen)
    return chosen


def put_left(out_ref, left, block):
    rows, rank = left.shape
    pieces = block // rank
    step = rows // pieces
    for p in range(pieces):
        out_ref[:step, p * rank : (p + 1) * rank] = left[p * step : (p + 1) * step]


def pack_kernel(bits_ref, w_ref, left_ref, right_ref, x_ref, g_ref, near_ref, far_ref, own_ref, self_ref):
    _, slots, rows, block = w_ref.shape
    sections = slots - 1
    rank_rows = right_ref.shape[1]
    flat = far_ref.shape[0] - x_ref.shape[0]
    near_ref[:rows] = slot_weights(bits_ref, w_ref, 0, sections)
    near_ref[rows : rows + rank_rows] = right_ref[0]
    near_ref[rows + rank_rows :] = g_ref[...]
    put_left(far_ref.at[:flat], left_ref[0], block)
    far_ref[flat:] = x_ref[...]
    self_ref[...] = w_ref[0, 0]
    for b in range(1, sections):
        own_ref[(b - 1) * rows : b * rows] = slot_weights(bits_ref, w_ref, b, sections)
    at = (sections - 1) * rows
    own_ref[at : at + rank_rows] = right_ref[0]
    put_left(own_ref.at[at + rank_rows :], left_ref[0], block)


def codes_of(x, g, far, near, low):
    lh, ll, rh, rl = low
    codes = nn(x, (lh[0], ll[0])) + nn(far, (lh[1], ll[1]))
    return codes, nt(g, (rh[0], rl[0])) + nt(near, (rh[1], rl[1]))


def put_rows(refs, value):
    at = 0
    for ref in refs:
        ref[...] = value[at : at + ref.shape[0]]
        at += ref.shape[0]


def sends_of(x, g, codes, code_grads, wide, low, outs):
    wh, wl = wide
    lh, ll, rh, rl = low
    last = wh.shape[0] - 1
    cuts = len(outs) // (last + 1)
    put_rows(outs[:cuts], nn(x, (wh[last], wl[last])) + nn(codes, (rh[1], rl[1])))
    for b in range(last):
        back = nt(g, (wh[b], wl[b]))
        if b == 0:
            back += nt(code_grads, (lh[1], ll[1]))
        put_rows(outs[(b + 1) * cuts : (b + 2) * cuts], back)


def messages(x_ref, g_ref, far_ref, near_ref, wide, low, outs):
    x, g = split(x_ref[...]), split(g_ref[...])
    codes, code_grads = codes_of(x, g, split(far_ref[...]), split(near_ref[...]), low)
    outs[0][...] = codes
    outs[1][...] = code_grads
    sends_of(x, g, split(codes), split(code_grads), wide, low, outs[2:])


def weights_kernel(sizes, *refs):
    sections, rows, rank_rows, rank, dp_count = sizes
    even_ref, odd_ref = refs[:2]
    early = refs[2:6] if sections == 2 else ()
    sh, sl, wh, wl, lh, ll, rh, rl, *outs = refs[2 + len(early) :]
    block = wh.shape[2]
    flat = rows * rank // block
    pieces = rows // flat
    me = lax.axis_index("dp")
    for k in range(dp_count):
        part = (odd_ref if k % 2 else even_ref).at[k // 2]
        owner = me ^ k
        at = 0

        def move(high_ref, low_ref, i, start, count, value):
            high, low = split(value)
            place = pl.ds(pl.multiple_of(start, 16), count)
            high_ref[i, place, :] = high
            low_ref[i, place, :] = low

        def move_wide(high_ref, low_ref, i, start, count):
            move(high_ref, low_ref, i, owner * count, count, part[start : start + count, :])
            return start + count

        def move_left(i, start):
            for p in range(pieces):
                value = part[start : start + flat, p * rank : (p + 1) * rank]
                move(lh, ll, i, owner * rows + p * flat, flat, value)
            return start + flat

        for i in range(sections - 1):
            at = move_wide(wh, wl, i, at, rows)
        at = move_wide(rh, rl, 0, at, rank_rows)
        at = move_left(0, at)
        at = move_wide(wh, wl, sections - 1, at, rows)
        at = move_wide(rh, rl, 1, at, rank_rows)
        at = move_left(1, at)
        at = move_wide(sh, sl, 0, at, rows)
    if early:
        messages(*early, (wh, wl), (lh, ll, rh, rl), outs)


def begin_kernel(x_ref, g_ref, wh, wl, lh, ll, rh, rl, c_ref, cg_ref, ahead_ref, back_ref):
    x, g = split(x_ref[...]), split(g_ref[...])
    c_ref[...] = nn(x, (lh[0], ll[0]))
    cg_ref[...] = nt(g, (rh[0], rl[0]))
    ahead_ref[...] = nn(x, (wh[1], wl[1]))
    back_ref[...] = nt(g, (wh[0], wl[0]))


def messages_kernel(far_ref, near_ref, lh, ll, rh, rl, *refs):
    c0_ref, cg0_ref, ahead0_ref, back0_ref, c_ref, cg_ref, ahead_ref, back_ref = refs
    codes = c0_ref[...] + nn(split(far_ref[...]), (lh[1], ll[1]))
    code_grads = cg0_ref[...] + nt(split(near_ref[...]), (rh[1], rl[1]))
    c_ref[...] = codes
    cg_ref[...] = code_grads
    ahead_ref[...] = ahead0_ref[...] + nn(split(codes), (rh[1], rl[1]))
    back_ref[...] = back0_ref[...] + nt(split(code_grads), (lh[1], ll[1]))


def codes_kernel(x_ref, g_ref, far_ref, near_ref, lh, ll, rh, rl, c_ref, cg_ref):
    parts = [split(r[...]) for r in (x_ref, g_ref, far_ref, near_ref)]
    c_ref[...], cg_ref[...] = codes_of(*parts, (lh, ll, rh, rl))


def sends_kernel(x_ref, g_ref, c_ref, cg_ref, wh, wl, lh, ll, rh, rl, *outs):
    parts = [split(r[...]) for r in (x_ref, g_ref, c_ref, cg_ref)]
    sends_of(*parts, (wh, wl), (lh, ll, rh, rl), outs)


def spread(dp_count, count, keep_refs, give_ref, put):
    me = lax.axis_index("dp")
    for k in range(dp_count):
        place = pl.ds(pl.multiple_of((me ^ k) * count, 8), count)
        put(give_ref.at[k // 2] if k % 2 else keep_refs[k // 2], place)


def self_kernel(sizes, scale, *refs):
    _, rows, _, _, dp_count = sizes
    x_ref, g_ref, *keep_refs, give_ref, dw = refs
    dw[...] = tn(split(x_ref[...]), split(g_ref[...])) * scale

    def put(out, place):
        out[...] = dw[place, :]

    spread(dp_count, rows, keep_refs, give_ref, put)


def cat(refs):
    values = [r[...] for r in refs]
    return values[0] if len(values) == 1 else jnp.concatenate(values, axis=0)


def take_pieces(refs, counts):
    groups, at = [], 0
    for count in counts:
        groups.append(cat(refs[at : at + count]))
        at += count
    return [split(group) for group in groups], refs[at:]


def grads_kernel(sizes, scale, counts, *refs):
    sections, rows, rank_rows, rank, dp_count = sizes
    (x, g, near, c, cg, *far), rest = take_pieces(refs, counts)
    half = dp_count // 2
    keep_refs = rest[:half]
    give_ref, dw, dr, dl = rest[half:]
    block = dw.shape[1]
    flat = rows * rank // block
    pieces = rows // flat
    at = [0]

    def spread_wide(source, count):
        def put(out, place):
            out[at[0] : at[0] + count, :] = source[place, :]

        spread(dp_count, count, keep_refs, give_ref, put)
        at[0] += count

    def spread_left(source):
        def put(out, place):
            value = source[place, :]
            for p in range(pieces):
                out[at[0] : at[0] + flat, p * rank : (p + 1) * rank] = value[
                    p * flat : (p + 1) * flat
                ]

        spread(dp_count, rows, keep_refs, give_ref, put)
        at[0] += flat

    dw[...] = tn(x, near) * scale
    spread_wide(dw, rows)
    dr[...] = tn(c, near) * scale
    spread_wide(dr, rank_rows)
    dl[...] = tn(far[0], cg) * scale
    spread_left(dl)
    for b in range(1, sections):
        dw[...] = tn(far[b - 1], g) * scale
        spread_wide(dw, rows)
    dr[...] = tn(c, g) * scale
    spread_wide(dr, rank_rows)
    dl[...] = tn(x, cg) * scale
    spread_left(dl)


def local_kernel(counts, *refs):
    (x, g, near, c, cg, *far), rest = take_pieces(refs, counts)
    sh, sl, wh, wl, lh, ll, rh, rl, *first, out_ref, grad_ref = rest
    last = wh.shape[0] - 1
    out = nn(x, (sh[0], sl[0])) + nn(c, (rh[0], rl[0]))
    for b in range(last):
        out += nn(far[b], (wh[b], wl[b]))
    out_ref[...] = out
    grad = nt(g, (sh[0], sl[0])) + nt(cg, (lh[0], ll[0]))
    grad_ref[...] = grad + nt(near, (wh[last], wl[last]))
    if first:
        ahead_ref, back_ref = first
        count = ahead_ref.shape[0]
        out_ref[:count] += ahead_ref[...]
        grad_ref[:count] += back_ref[...]


def join_kernel(whole_ref, late_ref, out_ref):
    early = whole_ref.shape[0] - late_ref.shape[0]
    out_ref[:early] = whole_ref[:early]
    out_ref[early:] = whole_ref[early:] + late_ref[...]


def place_kernel(sizes, *refs):
    sections, rows, rank_rows, rank, _ = sizes
    bits_ref, self_ref, kept_ref, near_ref, far_ref, w_ref, left_ref, right_ref = refs
    block = kept_ref.shape[1]
    flat = rows * rank // block
    pieces = rows // flat
    w_ref[0, 0] = self_ref[...]
    for s in range(sections):
        chosen = near_ref[:rows]
        for b in range(1, sections):
            chosen = jnp.where(bits_ref[0, s] == b, kept_ref[(b - 1) * rows : b * rows], chosen)
        w_ref[0, 1 + s] = chosen
    at = (sections - 1) * rows
    right_ref[0] = kept_ref[at : at + rank_rows] + near_ref[rows:]
    at += rank_rows
    for p in range(pieces):
        columns = slice(p * rank, (p + 1) * rank)
        left_ref[0, p * flat : (p + 1) * flat, :] = (
            kept_ref[at : at + flat, columns] + far_ref[:, columns]
        )


def on_device(inputs, partner_bits, block_weights, low_left, low_right, cotangent):
    tokens, block = inputs.shape
    sections = partner_bits.shape[1]
    dp_count = lax.axis_size("dp")
    half = dp_count // 2
    rows, rank = low_left.shape[1:]
    rank_rows = low_right.shape[1]
    all_rank = rank_rows * dp_count
    flat = rows * rank // block
    sizes = (sections, rows, rank_rows, rank, dp_count)
    early = tokens * EARLY // 512 // 16 * 16
    late = tokens - early
    lent_rows = rows + rank_rows
    own_rows = sections * rows + rank_rows + flat
    sum_rows = own_rows + lent_rows + flat - rows
    smem = pl.BlockSpec(memory_space=pltpu.SMEM)
    vmem = pl.BlockSpec(memory_space=pltpu.VMEM)
    usual = partner_bits[0, 0] >= 0
    folds = sections == 2
    scale = 1.0 / math.sqrt(tokens * dp_count)

    by_slot = jnp.transpose(block_weights, (0, 2, 1, 3))
    pack_shapes = [(lent_rows + early, block), (flat + early, block), (own_rows - rows, block), (rows, block)]
    out_near, out_far, own, own_self = call(
        pack_kernel,
        [f32(*s) for s in pack_shapes],
        [partner_bits, by_slot, low_left, low_right, inputs, cotangent],
        grid=(1,),
        in_specs=[
            smem, whole(by_slot.shape), whole(low_left.shape), whole(low_right.shape),
            whole((early, block)), whole((early, block)),
        ],
        out_specs=[whole(s) for s in pack_shapes],
        vmem_bytes=PACK_VMEM_BYTES,
    )
    got_near = across(out_near, "feat", 1)
    got_far = across(out_far, "feat", 2)
    own = [own] + [across(own, "dp", k) for k in range(2, dp_count, 2)]
    late_x, got_far = lax.optimization_barrier((inputs[early:], got_far))
    late_far = across(late_x, "feat", 2)
    late_g, got_near = lax.optimization_barrier((cotangent[early:], got_near))
    late_near = across(late_g, "feat", 1)
    early_far, early_near = got_far[flat:], got_near[lent_rows:]
    lent = jnp.concatenate([got_near[:lent_rows], got_far[:flat], own_self])
    lent, own = lax.optimization_barrier((lent, own))
    lent = gather_rows(lent, dp_count)
    *self_keep, self_give = call(
        functools.partial(self_kernel, sizes, scale),
        [f32(rows, block)] * half + [f32(half, rows, block)],
        [inputs, cotangent],
        scratch=[pltpu.VMEM((block, block), F32)],
    )

    s_shape = (1, block, block)
    w_shape = (sections, block, block)
    l_shape = (2, block, rank)
    r_shape = (2, all_rank, block)
    shapes = [s_shape, s_shape, w_shape, w_shape, l_shape, l_shape, r_shape, r_shape]

    def message_shapes(*cuts):
        sends = [(cut, block) for cut in cuts] * sections
        return [(sum(cuts), rank)] * 2 + sends

    made = [b16(*s) for s in shapes]
    if folds:
        made += [f32(*s) for s in message_shapes(early)]

    def prepare(own, lent, keep, give, *early_parts):
        even = jnp.stack([jnp.concatenate(pair) for pair in zip(own, lent)])
        odd = across(even, "dp", 1)
        got = across(give, "dp", 1)
        got, odd = lax.optimization_barrier((got, odd))
        self_grads = keep[0] + got[0]
        for m in range(1, half):
            self_grads = self_grads + across(keep[m] + got[m], "dp", 2 * m)
        operands = [even, odd, *early_parts] if folds else [even, odd]
        return self_grads, *(
            call(
                functools.partial(weights_kernel, sizes),
                made,
                operands,
                grid=(1,),
                in_specs=[whole(even.shape)] * 2 + [whole((early, block))] * (len(operands) - 2),
                out_specs=[whole(s.shape) for s in made],
            )
        )

    def empty(*_):
        return tuple(jnp.zeros(s.shape, s.dtype) for s in [f32(rows, block)] + made)

    self_grads, *weights = lax.cond(
        usual, prepare, empty,
        own, lent, self_keep, self_give, inputs, cotangent, early_far, early_near,
    )
    weights, sent = weights[:8], weights[8:]
    weight_specs = [whole(s) for s in shapes]
    near = [early_near, late_near]
    far = [[early_far, late_far]]
    if folds:
        late_shapes = message_shapes(late)
        step = late // 2 if late % 32 == 0 else late
        late_specs = [by_tokens(step, width) for _, width in late_shapes]
        begun = call(
            begin_kernel,
            [f32(*s) for s in late_shapes],
            [late_x, late_g, *weights[2:]],
            grid=(late // step,),
            in_specs=[by_tokens(step, block)] * 2 + weight_specs[2:],
            out_specs=late_specs,
        )
        late_sent = call(
            messages_kernel,
            [f32(*s) for s in late_shapes],
            [late_far, late_near, *weights[4:], *begun],
            grid=(late // step,),
            in_specs=[by_tokens(step, block)] * 2 + weight_specs[4:] + late_specs,
            out_specs=late_specs,
        )
        first = [across(part, "feat", 1 << b) for b, part in enumerate(sent[2:])]
        rest = list(late_sent[2:])
        rest[0], first = lax.optimization_barrier((rest[0], first))
        first, late_sent = lax.optimization_barrier((first, late_sent))
        rest = [across(part, "feat", 1 << b) for b, part in enumerate(rest)]
        codes, code_grads = ([sent[i], late_sent[i]] for i in range(2))
    else:
        far += [[across(inputs, "feat", 1 << b)] for b in range(2, sections)]
        step = tokens // 2
        wide, thin = by_tokens(step, block), by_tokens(step, rank)
        codes, code_grads = call(
            codes_kernel,
            [f32(tokens, rank)] * 2,
            [inputs, cotangent, jnp.concatenate(far[0]), jnp.concatenate(near), *weights[4:]],
            grid=(2,),
            in_specs=[wide] * 4 + weight_specs[4:],
            out_specs=[thin, thin],
        )
        for b in range(2, sections):
            codes = codes + across(codes, "feat", 1 << b)
            code_grads = code_grads + across(code_grads, "feat", 1 << b)
        messages = call(
            sends_kernel,
            [f32(tokens, block)] * sections,
            [inputs, cotangent, codes, code_grads, *weights[2:]],
            grid=(2,),
            in_specs=[wide, wide, thin, thin, *weight_specs[2:]],
            out_specs=[wide] * sections,
        )
        messages = [across(part, "feat", 1 << b) for b, part in enumerate(messages)]
        codes, code_grads = [codes], [code_grads]

    groups = [[inputs], [cotangent], near, codes, code_grads, *far]
    counts = [len(group) for group in groups]

    def finish(groups, weights, first):
        *keep, give = call(
            functools.partial(grads_kernel, sizes, scale, counts),
            [f32(sum_rows, block)] * half + [f32(half, sum_rows, block)],
            [part for group in groups for part in group],
            scratch=[
                pltpu.VMEM((block, block), F32),
                pltpu.VMEM((all_rank, block), F32),
                pltpu.VMEM((block, rank), F32),
            ],
        )
        groups, give = lax.optimization_barrier((groups, give))
        got = across(give, "dp", 1)
        beside = call(
            functools.partial(local_kernel, counts),
            [f32(tokens, block)] * 2,
            [part for group in groups for part in group] + weights + first,
        )
        total, (out, grad) = scatter_rows([keep[m] + got[m] for m in range(half)], beside)
        at = lent_rows + flat
        return out, grad, total[:lent_rows], total[lent_rows:at], total[at:]

    def nothing(*_):
        shapes = [(tokens, block)] * 2 + [(n, block) for n in (lent_rows, flat, own_rows - rows)]
        return tuple(jnp.zeros(shape, F32) for shape in shapes)

    outputs, grad, near_back, far_back, kept = lax.cond(
        usual, finish, nothing, groups, weights, first if folds else []
    )
    near_back = across(near_back, "feat", 1)
    far_back = across(far_back, "feat", 2)
    if folds:
        outputs, grad = (
            call(join_kernel, [f32(tokens, block)], parts, vmem_bytes=JOIN_VMEM_BYTES)[0]
            for parts in zip((outputs, grad), rest)
        )
    else:
        outputs = outputs + messages[0]
        for part in messages[1:]:
            grad = grad + part
    outputs, grad, kept = lax.optimization_barrier((outputs, grad, kept))
    block_grads, left_grads, right_grads = call(
        functools.partial(place_kernel, sizes),
        [f32(*by_slot.shape), f32(*low_left.shape), f32(*low_right.shape)],
        [partner_bits, self_grads, kept, near_back, far_back],
        in_specs=[smem] + [vmem] * 4,
    )
    block_grads = jnp.transpose(block_grads, (0, 2, 1, 3))
    return (outputs, grad, block_grads, left_grads, right_grads)


def solution(mesh):
    in_specs = (
        P("dp", "feat"),
        P("feat", None),
        P("feat", "dp", None, None),
        P("feat", "dp", None),
        P("feat", "dp", None),
        P("dp", "feat"),
    )
    out_specs = (
        P("dp", "feat"),
        P("dp", "feat"),
        P("feat", "dp", None, None),
        P("feat", "dp", None),
        P("feat", "dp", None),
    )
    return jax.shard_map(
        on_device, mesh=mesh, in_specs=in_specs, out_specs=out_specs, check_vma=False
    )
```

```python
import functools
import math

import jax
import jax.numpy as jnp
from jax import lax
from jax.experimental import pallas as pl
from jax.experimental.pallas import tpu as pltpu
from jax.sharding import PartitionSpec as P

F32 = jnp.float32
BF16 = jnp.bfloat16
EARLY = 48
VMEM_BYTES = 20 * 1024 * 1024
JOIN_VMEM_BYTES = 8 * 1024 * 1024
PACK_VMEM_BYTES = 60 * 1024 * 1024


def across(block, axis, apart):
    count = lax.axis_size(axis)
    return lax.ppermute(block, axis, [(i, i ^ apart) for i in range(count)])


def scatter_rows(blocks, beside):
    bits = len(blocks).bit_length() - 1
    if not bits:
        return blocks[0], beside
    rows = blocks[0].shape[0]
    cuts = [rows * g // bits // 8 * 8 for g in range(bits)] + [rows]
    groups = [
        {m: block[cuts[g] : cuts[g + 1]] for m, block in enumerate(blocks)} for g in range(bits)
    ]
    for step in range(bits):
        turn = [(g + step) % bits for g in range(bits)]
        sent = [[m for m in group if m >> bit & 1] for group, bit in zip(groups, turn)]
        stacks = [jnp.stack([group[m] for m in ms]) for group, ms in zip(groups, sent)]
        stacks = lax.optimization_barrier(stacks)
        got = [across(stack, "dp", 2 << bit) for stack, bit in zip(stacks, turn)]
        got, beside = lax.optimization_barrier((got, beside))
        groups = [
            {m ^ 1 << bit: group[m ^ 1 << bit] + part[i] for i, m in enumerate(ms)}
            for group, ms, part, bit in zip(groups, sent, got, turn)
        ]
    return jnp.concatenate([group[0] for group in groups]), beside


def gather_rows(part, count):
    bits = (count // 2).bit_length() - 1
    if not bits:
        return [part]
    rows = part.shape[0]
    cuts = [rows * g // bits // 8 * 8 for g in range(bits)] + [rows]
    groups = [{0: part[cuts[g] : cuts[g + 1]]} for g in range(bits)]
    for step in range(bits):
        turn = [(g + step) % bits for g in range(bits)]
        stacks = [jnp.stack([group[m] for m in sorted(group)]) for group in groups]
        got = [across(stack, "dp", 2 << bit) for stack, bit in zip(stacks, turn)]
        got = lax.optimization_barrier(got)
        groups = [
            {**group, **{m ^ 1 << bit: more[i] for i, m in enumerate(sorted(group))}}
            for group, more, bit in zip(groups, got, turn)
        ]
    return [jnp.concatenate([group[m] for group in groups]) for m in range(count // 2)]


def split(value):
    high = value.astype(BF16)
    return high, (value - high.astype(F32)).astype(BF16)


def dot3(left, right, over):
    def one(a, b):
        return lax.dot_general(
            a, b, ((over[:1], over[1:]), ((), ())), preferred_element_type=F32
        )

    return one(left[0], right[0]) + (one(left[0], right[1]) + one(left[1], right[0]))


def nn(left, right):
    return dot3(left, right, (1, 0))


def nt(left, right):
    return dot3(left, right, (1, 1))


def tn(left, right):
    return dot3(left, right, (0, 0))


def call(
    kernel, out_shapes, operands, grid=None, in_specs=None, out_specs=None, scratch=(),
    vmem_bytes=VMEM_BYTES,
):
    vmem = pl.BlockSpec(memory_space=pltpu.VMEM)
    kwargs = {}
    if grid is None:
        in_specs = in_specs or [vmem] * len(operands)
        out_specs = [vmem] * len(out_shapes)
    else:
        kwargs["grid"] = grid
    return pl.pallas_call(
        kernel,
        out_shape=out_shapes,
        in_specs=in_specs,
        out_specs=out_specs,
        scratch_shapes=list(scratch),
        cost_estimate=pl.CostEstimate(flops=1, bytes_accessed=1, transcendentals=0),
        compiler_params=pltpu.CompilerParams(vmem_limit_bytes=vmem_bytes),
        **kwargs,
    )(*operands)


def f32(*shape):
    return jax.ShapeDtypeStruct(shape, F32)


def b16(*shape):
    return jax.ShapeDtypeStruct(shape, BF16)


def whole(shape):
    return pl.BlockSpec(shape, lambda *_: (0,) * len(shape))


def by_tokens(tokens, width):
    return pl.BlockSpec((tokens, width), lambda i: (i, 0))


def slot_weights(bits_ref, w_ref, bit, sections):
    chosen = w_ref[0, sections]
    for s in range(sections - 1):
        chosen = jnp.where(bits_ref[0, s] == bit, w_ref[0, 1 + s], chosen)
    return chosen


def put_left(out_ref, left, block):
    rows, rank = left.shape
    pieces = block // rank
    step = rows // pieces
    for p in range(pieces):
        out_ref[:step, p * rank : (p + 1) * rank] = left[p * step : (p + 1) * step]


def pack_kernel(bits_ref, w_ref, left_ref, right_ref, x_ref, g_ref, near_ref, far_ref, own_ref, self_ref):
    _, slots, rows, block = w_ref.shape
    sections = slots - 1
    rank_rows = right_ref.shape[1]
    flat = far_ref.shape[0] - x_ref.shape[0]
    near_ref[:rows] = slot_weights(bits_ref, w_ref, 0, sections)
    near_ref[rows : rows + rank_rows] = right_ref[0]
    near_ref[rows + rank_rows :] = g_ref[...]
    put_left(far_ref.at[:flat], left_ref[0], block)
    far_ref[flat:] = x_ref[...]
    self_ref[...] = w_ref[0, 0]
    for b in range(1, sections):
        own_ref[(b - 1) * rows : b * rows] = slot_weights(bits_ref, w_ref, b, sections)
    at = (sections - 1) * rows
    own_ref[at : at + rank_rows] = right_ref[0]
    put_left(own_ref.at[at + rank_rows :], left_ref[0], block)


def codes_of(x, g, far, near, low):
    lh, ll, rh, rl = low
    codes = nn(x, (lh[0], ll[0])) + nn(far, (lh[1], ll[1]))
    return codes, nt(g, (rh[0], rl[0])) + nt(near, (rh[1], rl[1]))


def put_rows(refs, value):
    at = 0
    for ref in refs:
        ref[...] = value[at : at + ref.shape[0]]
        at += ref.shape[0]


def sends_of(x, g, codes, code_grads, wide, low, outs):
    wh, wl = wide
    lh, ll, rh, rl = low
    last = wh.shape[0] - 1
    cuts = len(outs) // (last + 1)
    put_rows(outs[:cuts], nn(x, (wh[last], wl[last])) + nn(codes, (rh[1], rl[1])))
    for b in range(last):
        back = nt(g, (wh[b], wl[b]))
        if b == 0:
            back += nt(code_grads, (lh[1], ll[1]))
        put_rows(outs[(b + 1) * cuts : (b + 2) * cuts], back)


def messages(x_ref, g_ref, far_ref, near_ref, wide, low, outs):
    x, g = split(x_ref[...]), split(g_ref[...])
    codes, code_grads = codes_of(x, g, split(far_ref[...]), split(near_ref[...]), low)
    outs[0][...] = codes
    outs[1][...] = code_grads
    sends_of(x, g, split(codes), split(code_grads), wide, low, outs[2:])


def weights_kernel(sizes, *refs):
    sections, rows, rank_rows, rank, dp_count = sizes
    even_ref, odd_ref = refs[:2]
    early = refs[2:6] if sections == 2 else ()
    sh, sl, wh, wl, lh, ll, rh, rl, *outs = refs[2 + len(early) :]
    block = wh.shape[2]
    flat = rows * rank // block
    pieces = rows // flat
    me = lax.axis_index("dp")
    for k in range(dp_count):
        part = (odd_ref if k % 2 else even_ref).at[k // 2]
        owner = me ^ k
        at = 0

        def move(high_ref, low_ref, i, start, count, value):
            high, low = split(value)
            place = pl.ds(pl.multiple_of(start, 16), count)
            high_ref[i, place, :] = high
            low_ref[i, place, :] = low

        def move_wide(high_ref, low_ref, i, start, count):
            move(high_ref, low_ref, i, owner * count, count, part[start : start + count, :])
            return start + count

        def move_left(i, start):
            for p in range(pieces):
                value = part[start : start + flat, p * rank : (p + 1) * rank]
                move(lh, ll, i, owner * rows + p * flat, flat, value)
            return start + flat

        for i in range(sections - 1):
            at = move_wide(wh, wl, i, at, rows)
        at = move_wide(rh, rl, 0, at, rank_rows)
        at = move_left(0, at)
        at = move_wide(wh, wl, sections - 1, at, rows)
        at = move_wide(rh, rl, 1, at, rank_rows)
        at = move_left(1, at)
        at = move_wide(sh, sl, 0, at, rows)
    if early:
        messages(*early, (wh, wl), (lh, ll, rh, rl), outs)


def begin_kernel(x_ref, g_ref, wh, wl, lh, ll, rh, rl, c_ref, cg_ref, ahead_ref, back_ref):
    x, g = split(x_ref[...]), split(g_ref[...])
    c_ref[...] = nn(x, (lh[0], ll[0]))
    cg_ref[...] = nt(g, (rh[0], rl[0]))
    ahead_ref[...] = nn(x, (wh[1], wl[1]))
    back_ref[...] = nt(g, (wh[0], wl[0]))


def messages_kernel(far_ref, near_ref, lh, ll, rh, rl, *refs):
    c0_ref, cg0_ref, ahead0_ref, back0_ref, c_ref, cg_ref, ahead_ref, back_ref = refs
    codes = c0_ref[...] + nn(split(far_ref[...]), (lh[1], ll[1]))
    code_grads = cg0_ref[...] + nt(split(near_ref[...]), (rh[1], rl[1]))
    c_ref[...] = codes
    cg_ref[...] = code_grads
    ahead_ref[...] = ahead0_ref[...] + nn(split(codes), (rh[1], rl[1]))
    back_ref[...] = back0_ref[...] + nt(split(code_grads), (lh[1], ll[1]))


def codes_kernel(x_ref, g_ref, far_ref, near_ref, lh, ll, rh, rl, c_ref, cg_ref):
    parts = [split(r[...]) for r in (x_ref, g_ref, far_ref, near_ref)]
    c_ref[...], cg_ref[...] = codes_of(*parts, (lh, ll, rh, rl))


def sends_kernel(x_ref, g_ref, c_ref, cg_ref, wh, wl, lh, ll, rh, rl, *outs):
    parts = [split(r[...]) for r in (x_ref, g_ref, c_ref, cg_ref)]
    sends_of(*parts, (wh, wl), (lh, ll, rh, rl), outs)


def spread(dp_count, count, keep_refs, give_ref, put):
    me = lax.axis_index("dp")
    for k in range(dp_count):
        place = pl.ds(pl.multiple_of((me ^ k) * count, 8), count)
        put(give_ref.at[k // 2] if k % 2 else keep_refs[k // 2], place)


def self_kernel(sizes, scale, *refs):
    _, rows, _, _, dp_count = sizes
    x_ref, g_ref, *keep_refs, give_ref, dw = refs
    dw[...] = tn(split(x_ref[...]), split(g_ref[...])) * scale

    def put(out, place):
        out[...] = dw[place, :]

    spread(dp_count, rows, keep_refs, give_ref, put)


def cat(refs):
    values = [r[...] for r in refs]
    return values[0] if len(values) == 1 else jnp.concatenate(values, axis=0)


def take_pieces(refs, counts):
    groups, at = [], 0
    for count in counts:
        groups.append(cat(refs[at : at + count]))
        at += count
    return [split(group) for group in groups], refs[at:]


def grads_kernel(sizes, scale, counts, *refs):
    sections, rows, rank_rows, rank, dp_count = sizes
    (x, g, near, c, cg, *far), rest = take_pieces(refs, counts)
    half = dp_count // 2
    keep_refs = rest[:half]
    give_ref, dw, dr, dl = rest[half:]
    block = dw.shape[1]
    flat = rows * rank // block
    pieces = rows // flat
    at = [0]

    def spread_wide(source, count):
        def put(out, place):
            out[at[0] : at[0] + count, :] = source[place, :]

        spread(dp_count, count, keep_refs, give_ref, put)
        at[0] += count

    def spread_left(source):
        def put(out, place):
            value = source[place, :]
            for p in range(pieces):
                out[at[0] : at[0] + flat, p * rank : (p + 1) * rank] = value[
                    p * flat : (p + 1) * flat
                ]

        spread(dp_count, rows, keep_refs, give_ref, put)
        at[0] += flat

    dw[...] = tn(x, near) * scale
    spread_wide(dw, rows)
    dr[...] = tn(c, near) * scale
    spread_wide(dr, rank_rows)
    dl[...] = tn(far[0], cg) * scale
    spread_left(dl)
    for b in range(1, sections):
        dw[...] = tn(far[b - 1], g) * scale
        spread_wide(dw, rows)
    dr[...] = tn(c, g) * scale
    spread_wide(dr, rank_rows)
    dl[...] = tn(x, cg) * scale
    spread_left(dl)


def local_kernel(counts, *refs):
    (x, g, near, c, cg, *far), rest = take_pieces(refs, counts)
    sh, sl, wh, wl, lh, ll, rh, rl, *first, out_ref, grad_ref = rest
    last = wh.shape[0] - 1
    out = nn(x, (sh[0], sl[0])) + nn(c, (rh[0], rl[0]))
    for b in range(last):
        out += nn(far[b], (wh[b], wl[b]))
    out_ref[...] = out
    grad = nt(g, (sh[0], sl[0])) + nt(cg, (lh[0], ll[0]))
    grad_ref[...] = grad + nt(near, (wh[last], wl[last]))
    if first:
        ahead_ref, back_ref = first
        count = ahead_ref.shape[0]
        out_ref[:count] += ahead_ref[...]
        grad_ref[:count] += back_ref[...]


def join_kernel(whole_ref, late_ref, out_ref):
    early = whole_ref.shape[0] - late_ref.shape[0]
    out_ref[:early] = whole_ref[:early]
    out_ref[early:] = whole_ref[early:] + late_ref[...]


def place_kernel(sizes, *refs):
    sections, rows, rank_rows, rank, _ = sizes
    bits_ref, self_ref, kept_ref, near_ref, far_ref, w_ref, left_ref, right_ref = refs
    block = kept_ref.shape[1]
    flat = rows * rank // block
    pieces = rows // flat
    w_ref[0, 0] = self_ref[...]
    for s in range(sections):
        chosen = near_ref[:rows]
        for b in range(1, sections):
            chosen = jnp.where(bits_ref[0, s] == b, kept_ref[(b - 1) * rows : b * rows], chosen)
        w_ref[0, 1 + s] = chosen
    at = (sections - 1) * rows
    right_ref[0] = kept_ref[at : at + rank_rows] + near_ref[rows:]
    at += rank_rows
    for p in range(pieces):
        columns = slice(p * rank, (p + 1) * rank)
        left_ref[0, p * flat : (p + 1) * flat, :] = (
            kept_ref[at : at + flat, columns] + far_ref[:, columns]
        )


def on_device(inputs, partner_bits, block_weights, low_left, low_right, cotangent):
    tokens, block = inputs.shape
    sections = partner_bits.shape[1]
    dp_count = lax.axis_size("dp")
    half = dp_count // 2
    rows, rank = low_left.shape[1:]
    rank_rows = low_right.shape[1]
    all_rank = rank_rows * dp_count
    flat = rows * rank // block
    sizes = (sections, rows, rank_rows, rank, dp_count)
    early = tokens * EARLY // 512 // 16 * 16
    late = tokens - early
    lent_rows = rows + rank_rows
    own_rows = sections * rows + rank_rows + flat
    sum_rows = own_rows + lent_rows + flat - rows
    smem = pl.BlockSpec(memory_space=pltpu.SMEM)
    vmem = pl.BlockSpec(memory_space=pltpu.VMEM)
    usual = partner_bits[0, 0] >= 0
    folds = sections == 2
    scale = 1.0 / math.sqrt(tokens * dp_count)

    by_slot = jnp.transpose(block_weights, (0, 2, 1, 3))
    pack_shapes = [(lent_rows + early, block), (flat + early, block), (own_rows - rows, block), (rows, block)]
    out_near, out_far, own, own_self = call(
        pack_kernel,
        [f32(*s) for s in pack_shapes],
        [partner_bits, by_slot, low_left, low_right, inputs, cotangent],
        grid=(1,),
        in_specs=[
            smem, whole(by_slot.shape), whole(low_left.shape), whole(low_right.shape),
            whole((early, block)), whole((early, block)),
        ],
        out_specs=[whole(s) for s in pack_shapes],
        vmem_bytes=PACK_VMEM_BYTES,
    )
    got_near = across(out_near, "feat", 1)
    got_far = across(out_far, "feat", 2)
    own = [own] + [across(own, "dp", k) for k in range(2, dp_count, 2)]
    late_x, got_far = lax.optimization_barrier((inputs[early:], got_far))
    late_far = across(late_x, "feat", 2)
    late_g, got_near = lax.optimization_barrier((cotangent[early:], got_near))
    late_near = across(late_g, "feat", 1)
    early_far, early_near = got_far[flat:], got_near[lent_rows:]
    lent = jnp.concatenate([got_near[:lent_rows], got_far[:flat], own_self])
    lent, own = lax.optimization_barrier((lent, own))
    lent = gather_rows(lent, dp_count)
    *self_keep, self_give = call(
        functools.partial(self_kernel, sizes, scale),
        [f32(rows, block)] * half + [f32(half, rows, block)],
        [inputs, cotangent],
        scratch=[pltpu.VMEM((block, block), F32)],
    )

    s_shape = (1, block, block)
    w_shape = (sections, block, block)
    l_shape = (2, block, rank)
    r_shape = (2, all_rank, block)
    shapes = [s_shape, s_shape, w_shape, w_shape, l_shape, l_shape, r_shape, r_shape]

    def message_shapes(*cuts):
        sends = [(cut, block) for cut in cuts] * sections
        return [(sum(cuts), rank)] * 2 + sends

    made = [b16(*s) for s in shapes]
    if folds:
        made += [f32(*s) for s in message_shapes(early)]

    def prepare(own, lent, keep, give, *early_parts):
        even = jnp.stack([jnp.concatenate(pair) for pair in zip(own, lent)])
        odd = across(even, "dp", 1)
        got = across(give, "dp", 1)
        got, odd = lax.optimization_barrier((got, odd))
        self_grads = keep[0] + got[0]
        for m in range(1, half):
            self_grads = self_grads + across(keep[m] + got[m], "dp", 2 * m)
        operands = [even, odd, *early_parts] if folds else [even, odd]
        return self_grads, *(
            call(
                functools.partial(weights_kernel, sizes),
                made,
                operands,
                grid=(1,),
                in_specs=[whole(even.shape)] * 2 + [whole((early, block))] * (len(operands) - 2),
                out_specs=[whole(s.shape) for s in made],
            )
        )

    def empty(*_):
        return tuple(jnp.zeros(s.shape, s.dtype) for s in [f32(rows, block)] + made)

    self_grads, *weights = lax.cond(
        usual, prepare, empty,
        own, lent, self_keep, self_give, inputs, cotangent, early_far, early_near,
    )
    weights, sent = weights[:8], weights[8:]
    weight_specs = [whole(s) for s in shapes]
    near = [early_near, late_near]
    far = [[early_far, late_far]]
    if folds:
        late_shapes = message_shapes(late)
        step = late // 2 if late % 32 == 0 else late
        late_specs = [by_tokens(step, width) for _, width in late_shapes]
        begun = call(
            begin_kernel,
            [f32(*s) for s in late_shapes],
            [late_x, late_g, *weights[2:]],
            grid=(late // step,),
            in_specs=[by_tokens(step, block)] * 2 + weight_specs[2:],
            out_specs=late_specs,
        )
        late_sent = call(
            messages_kernel,
            [f32(*s) for s in late_shapes],
            [late_far, late_near, *weights[4:], *begun],
            grid=(late // step,),
            in_specs=[by_tokens(step, block)] * 2 + weight_specs[4:] + late_specs,
            out_specs=late_specs,
        )
        first = [across(part, "feat", 1 << b) for b, part in enumerate(sent[2:])]
        rest = list(late_sent[2:])
        rest[1], first = lax.optimization_barrier((rest[1], first))
        first, late_sent = lax.optimization_barrier((first, late_sent))
        rest = [across(part, "feat", 1 << b) for b, part in enumerate(rest)]
        codes, code_grads = ([sent[i], late_sent[i]] for i in range(2))
    else:
        far += [[across(inputs, "feat", 1 << b)] for b in range(2, sections)]
        step = tokens // 2
        wide, thin = by_tokens(step, block), by_tokens(step, rank)
        codes, code_grads = call(
            codes_kernel,
            [f32(tokens, rank)] * 2,
            [inputs, cotangent, jnp.concatenate(far[0]), jnp.concatenate(near), *weights[4:]],
            grid=(2,),
            in_specs=[wide] * 4 + weight_specs[4:],
            out_specs=[thin, thin],
        )
        for b in range(2, sections):
            codes = codes + across(codes, "feat", 1 << b)
            code_grads = code_grads + across(code_grads, "feat", 1 << b)
        messages = call(
            sends_kernel,
            [f32(tokens, block)] * sections,
            [inputs, cotangent, codes, code_grads, *weights[2:]],
            grid=(2,),
            in_specs=[wide, wide, thin, thin, *weight_specs[2:]],
            out_specs=[wide] * sections,
        )
        messages = [across(part, "feat", 1 << b) for b, part in enumerate(messages)]
        codes, code_grads = [codes], [code_grads]

    groups = [[inputs], [cotangent], near, codes, code_grads, *far]
    counts = [len(group) for group in groups]

    def finish(groups, weights, first):
        *keep, give = call(
            functools.partial(grads_kernel, sizes, scale, counts),
            [f32(sum_rows, block)] * half + [f32(half, sum_rows, block)],
            [part for group in groups for part in group],
            scratch=[
                pltpu.VMEM((block, block), F32),
                pltpu.VMEM((all_rank, block), F32),
                pltpu.VMEM((block, rank), F32),
            ],
        )
        groups, give = lax.optimization_barrier((groups, give))
        got = across(give, "dp", 1)
        beside = call(
            functools.partial(local_kernel, counts),
            [f32(tokens, block)] * 2,
            [part for group in groups for part in group] + weights + first,
        )
        total, (out, grad) = scatter_rows([keep[m] + got[m] for m in range(half)], beside)
        at = lent_rows + flat
        return out, grad, total[:lent_rows], total[lent_rows:at], total[at:]

    def nothing(*_):
        shapes = [(tokens, block)] * 2 + [(n, block) for n in (lent_rows, flat, own_rows - rows)]
        return tuple(jnp.zeros(shape, F32) for shape in shapes)

    outputs, grad, near_back, far_back, kept = lax.cond(
        usual, finish, nothing, groups, weights, first if folds else []
    )
    near_back = across(near_back, "feat", 1)
    far_back = across(far_back, "feat", 2)
    if folds:
        outputs, grad = (
            call(join_kernel, [f32(tokens, block)], parts, vmem_bytes=JOIN_VMEM_BYTES)[0]
            for parts in zip((outputs, grad), rest)
        )
    else:
        outputs = outputs + messages[0]
        for part in messages[1:]:
            grad = grad + part
    outputs, grad, kept = lax.optimization_barrier((outputs, grad, kept))
    block_grads, left_grads, right_grads = call(
        functools.partial(place_kernel, sizes),
        [f32(*by_slot.shape), f32(*low_left.shape), f32(*low_right.shape)],
        [partner_bits, self_grads, kept, near_back, far_back],
        in_specs=[smem] + [vmem] * 4,
    )
    block_grads = jnp.transpose(block_grads, (0, 2, 1, 3))
    return (outputs, grad, block_grads, left_grads, right_grads)


def solution(mesh):
    in_specs = (
        P("dp", "feat"),
        P("feat", None),
        P("feat", "dp", None, None),
        P("feat", "dp", None),
        P("feat", "dp", None),
        P("dp", "feat"),
    )
    out_specs = (
        P("dp", "feat"),
        P("dp", "feat"),
        P("feat", "dp", None, None),
        P("feat", "dp", None),
        P("feat", "dp", None),
    )
    return jax.shard_map(
        on_device, mesh=mesh, in_specs=in_specs, out_specs=out_specs, check_vma=False
    )
```

```python
import functools
import math

import jax
import jax.numpy as jnp
from jax import lax
from jax.experimental import pallas as pl
from jax.experimental.pallas import tpu as pltpu
from jax.sharding import PartitionSpec as P

F32 = jnp.float32
BF16 = jnp.bfloat16
EARLY = 48
VMEM_BYTES = 20 * 1024 * 1024
JOIN_VMEM_BYTES = 8 * 1024 * 1024
PACK_VMEM_BYTES = 60 * 1024 * 1024


def across(block, axis, apart):
    count = lax.axis_size(axis)
    return lax.ppermute(block, axis, [(i, i ^ apart) for i in range(count)])


def scatter_rows(blocks, beside):
    bits = len(blocks).bit_length() - 1
    if not bits:
        return blocks[0], beside
    rows = blocks[0].shape[0]
    cuts = [rows * g // bits // 8 * 8 for g in range(bits)] + [rows]
    groups = [
        {m: block[cuts[g] : cuts[g + 1]] for m, block in enumerate(blocks)} for g in range(bits)
    ]
    for step in range(bits):
        turn = [(g + step) % bits for g in range(bits)]
        sent = [[m for m in group if m >> bit & 1] for group, bit in zip(groups, turn)]
        stacks = [jnp.stack([group[m] for m in ms]) for group, ms in zip(groups, sent)]
        stacks = lax.optimization_barrier(stacks)
        got = [across(stack, "dp", 2 << bit) for stack, bit in zip(stacks, turn)]
        got, beside = lax.optimization_barrier((got, beside))
        groups = [
            {m ^ 1 << bit: group[m ^ 1 << bit] + part[i] for i, m in enumerate(ms)}
            for group, ms, part, bit in zip(groups, sent, got, turn)
        ]
    return jnp.concatenate([group[0] for group in groups]), beside


def gather_rows(part, count):
    bits = (count // 2).bit_length() - 1
    if not bits:
        return [part]
    rows = part.shape[0]
    cuts = [rows * g // bits // 8 * 8 for g in range(bits)] + [rows]
    groups = [{0: part[cuts[g] : cuts[g + 1]]} for g in range(bits)]
    for step in range(bits):
        turn = [(g + step) % bits for g in range(bits)]
        stacks = [jnp.stack([group[m] for m in sorted(group)]) for group in groups]
        got = [across(stack, "dp", 2 << bit) for stack, bit in zip(stacks, turn)]
        got = lax.optimization_barrier(got)
        groups = [
            {**group, **{m ^ 1 << bit: more[i] for i, m in enumerate(sorted(group))}}
            for group, more, bit in zip(groups, got, turn)
        ]
    return [jnp.concatenate([group[m] for group in groups]) for m in range(count // 2)]


def split(value):
    high = value.astype(BF16)
    return high, (value - high.astype(F32)).astype(BF16)


def dot3(left, right, over):
    def one(a, b):
        return lax.dot_general(
            a, b, ((over[:1], over[1:]), ((), ())), preferred_element_type=F32
        )

    return one(left[0], right[0]) + (one(left[0], right[1]) + one(left[1], right[0]))


def nn(left, right):
    return dot3(left, right, (1, 0))


def nt(left, right):
    return dot3(left, right, (1, 1))


def tn(left, right):
    return dot3(left, right, (0, 0))


def call(
    kernel, out_shapes, operands, grid=None, in_specs=None, out_specs=None, scratch=(),
    vmem_bytes=VMEM_BYTES,
):
    vmem = pl.BlockSpec(memory_space=pltpu.VMEM)
    kwargs = {}
    if grid is None:
        in_specs = in_specs or [vmem] * len(operands)
        out_specs = [vmem] * len(out_shapes)
    else:
        kwargs["grid"] = grid
    return pl.pallas_call(
        kernel,
        out_shape=out_shapes,
        in_specs=in_specs,
        out_specs=out_specs,
        scratch_shapes=list(scratch),
        cost_estimate=pl.CostEstimate(flops=1, bytes_accessed=1, transcendentals=0),
        compiler_params=pltpu.CompilerParams(vmem_limit_bytes=vmem_bytes),
        **kwargs,
    )(*operands)


def f32(*shape):
    return jax.ShapeDtypeStruct(shape, F32)


def b16(*shape):
    return jax.ShapeDtypeStruct(shape, BF16)


def whole(shape):
    return pl.BlockSpec(shape, lambda *_: (0,) * len(shape))


def by_tokens(tokens, width):
    return pl.BlockSpec((tokens, width), lambda i: (i, 0))


def slot_weights(bits_ref, w_ref, bit, sections):
    chosen = w_ref[0, sections]
    for s in range(sections - 1):
        chosen = jnp.where(bits_ref[0, s] == bit, w_ref[0, 1 + s], chosen)
    return chosen


def put_left(out_ref, left, block):
    rows, rank = left.shape
    pieces = block // rank
    step = rows // pieces
    for p in range(pieces):
        out_ref[:step, p * rank : (p + 1) * rank] = left[p * step : (p + 1) * step]


def pack_kernel(bits_ref, w_ref, left_ref, right_ref, x_ref, g_ref, near_ref, far_ref, own_ref, self_ref):
    _, slots, rows, block = w_ref.shape
    sections = slots - 1
    rank_rows = right_ref.shape[1]
    flat = far_ref.shape[0] - x_ref.shape[0]
    near_ref[:rows] = slot_weights(bits_ref, w_ref, 0, sections)
    near_ref[rows : rows + rank_rows] = right_ref[0]
    near_ref[rows + rank_rows :] = g_ref[...]
    put_left(far_ref.at[:flat], left_ref[0], block)
    far_ref[flat:] = x_ref[...]
    self_ref[...] = w_ref[0, 0]
    for b in range(1, sections):
        own_ref[(b - 1) * rows : b * rows] = slot_weights(bits_ref, w_ref, b, sections)
    at = (sections - 1) * rows
    own_ref[at : at + rank_rows] = right_ref[0]
    put_left(own_ref.at[at + rank_rows :], left_ref[0], block)


def codes_of(x, g, far, near, low):
    lh, ll, rh, rl = low
    codes = nn(x, (lh[0], ll[0])) + nn(far, (lh[1], ll[1]))
    return codes, nt(g, (rh[0], rl[0])) + nt(near, (rh[1], rl[1]))


def put_rows(refs, value):
    at = 0
    for ref in refs:
        ref[...] = value[at : at + ref.shape[0]]
        at += ref.shape[0]


def sends_of(x, g, codes, code_grads, wide, low, outs):
    wh, wl = wide
    lh, ll, rh, rl = low
    last = wh.shape[0] - 1
    cuts = len(outs) // (last + 1)
    put_rows(outs[:cuts], nn(x, (wh[last], wl[last])) + nn(codes, (rh[1], rl[1])))
    for b in range(last):
        back = nt(g, (wh[b], wl[b]))
        if b == 0:
            back += nt(code_grads, (lh[1], ll[1]))
        put_rows(outs[(b + 1) * cuts : (b + 2) * cuts], back)


def messages(x_ref, g_ref, far_ref, near_ref, wide, low, outs):
    x, g = split(x_ref[...]), split(g_ref[...])
    codes, code_grads = codes_of(x, g, split(far_ref[...]), split(near_ref[...]), low)
    outs[0][...] = codes
    outs[1][...] = code_grads
    sends_of(x, g, split(codes), split(code_grads), wide, low, outs[2:])


def weights_kernel(sizes, *refs):
    sections, rows, rank_rows, rank, dp_count = sizes
    even_ref, odd_ref = refs[:2]
    early = refs[2:6] if sections == 2 else ()
    sh, sl, wh, wl, lh, ll, rh, rl, *outs = refs[2 + len(early) :]
    block = wh.shape[2]
    flat = rows * rank // block
    pieces = rows // flat
    me = lax.axis_index("dp")
    for k in range(dp_count):
        part = (odd_ref if k % 2 else even_ref).at[k // 2]
        owner = me ^ k
        at = 0

        def move(high_ref, low_ref, i, start, count, value):
            high, low = split(value)
            place = pl.ds(pl.multiple_of(start, 16), count)
            high_ref[i, place, :] = high
            low_ref[i, place, :] = low

        def move_wide(high_ref, low_ref, i, start, count):
            move(high_ref, low_ref, i, owner * count, count, part[start : start + count, :])
            return start + count

        def move_left(i, start):
            for p in range(pieces):
                value = part[start : start + flat, p * rank : (p + 1) * rank]
                move(lh, ll, i, owner * rows + p * flat, flat, value)
            return start + flat

        for i in range(sections - 1):
            at = move_wide(wh, wl, i, at, rows)
        at = move_wide(rh, rl, 0, at, rank_rows)
        at = move_left(0, at)
        at = move_wide(wh, wl, sections - 1, at, rows)
        at = move_wide(rh, rl, 1, at, rank_rows)
        at = move_left(1, at)
        at = move_wide(sh, sl, 0, at, rows)
    if early:
        messages(*early, (wh, wl), (lh, ll, rh, rl), outs)


def begin_kernel(x_ref, g_ref, wh, wl, lh, ll, rh, rl, c_ref, cg_ref, ahead_ref, back_ref):
    x, g = split(x_ref[...]), split(g_ref[...])
    c_ref[...] = nn(x, (lh[0], ll[0]))
    cg_ref[...] = nt(g, (rh[0], rl[0]))
    ahead_ref[...] = nn(x, (wh[1], wl[1]))
    back_ref[...] = nt(g, (wh[0], wl[0]))


def messages_kernel(far_ref, near_ref, lh, ll, rh, rl, *refs):
    c0_ref, cg0_ref, ahead0_ref, back0_ref, c_ref, cg_ref, ahead_ref, back_ref = refs
    codes = c0_ref[...] + nn(split(far_ref[...]), (lh[1], ll[1]))
    code_grads = cg0_ref[...] + nt(split(near_ref[...]), (rh[1], rl[1]))
    c_ref[...] = codes
    cg_ref[...] = code_grads
    ahead_ref[...] = ahead0_ref[...] + nn(split(codes), (rh[1], rl[1]))
    back_ref[...] = back0_ref[...] + nt(split(code_grads), (lh[1], ll[1]))


def codes_kernel(x_ref, g_ref, far_ref, near_ref, lh, ll, rh, rl, c_ref, cg_ref):
    parts = [split(r[...]) for r in (x_ref, g_ref, far_ref, near_ref)]
    c_ref[...], cg_ref[...] = codes_of(*parts, (lh, ll, rh, rl))


def sends_kernel(x_ref, g_ref, c_ref, cg_ref, wh, wl, lh, ll, rh, rl, *outs):
    parts = [split(r[...]) for r in (x_ref, g_ref, c_ref, cg_ref)]
    sends_of(*parts, (wh, wl), (lh, ll, rh, rl), outs)


def spread(dp_count, count, keep_refs, give_ref, put):
    me = lax.axis_index("dp")
    for k in range(dp_count):
        place = pl.ds(pl.multiple_of((me ^ k) * count, 8), count)
        put(give_ref.at[k // 2] if k % 2 else keep_refs[k // 2], place)


def self_kernel(sizes, scale, *refs):
    _, rows, _, _, dp_count = sizes
    x_ref, g_ref, *keep_refs, give_ref, dw = refs
    dw[...] = tn(split(x_ref[...]), split(g_ref[...])) * scale

    def put(out, place):
        out[...] = dw[place, :]

    spread(dp_count, rows, keep_refs, give_ref, put)


def cat(refs):
    values = [r[...] for r in refs]
    return values[0] if len(values) == 1 else jnp.concatenate(values, axis=0)


def take_pieces(refs, counts):
    groups, at = [], 0
    for count in counts:
        groups.append(cat(refs[at : at + count]))
        at += count
    return [split(group) for group in groups], refs[at:]


def grads_kernel(sizes, scale, counts, *refs):
    sections, rows, rank_rows, rank, dp_count = sizes
    (x, g, near, c, cg, *far), rest = take_pieces(refs, counts)
    half = dp_count // 2
    keep_refs = rest[:half]
    give_ref, dw, dr, dl = rest[half:]
    block = dw.shape[1]
    flat = rows * rank // block
    pieces = rows // flat
    at = [0]

    def spread_wide(source, count):
        def put(out, place):
            out[at[0] : at[0] + count, :] = source[place, :]

        spread(dp_count, count, keep_refs, give_ref, put)
        at[0] += count

    def spread_left(source):
        def put(out, place):
            value = source[place, :]
            for p in range(pieces):
                out[at[0] : at[0] + flat, p * rank : (p + 1) * rank] = value[
                    p * flat : (p + 1) * flat
                ]

        spread(dp_count, rows, keep_refs, give_ref, put)
        at[0] += flat

    dw[...] = tn(x, near) * scale
    spread_wide(dw, rows)
    dr[...] = tn(c, near) * scale
    spread_wide(dr, rank_rows)
    dl[...] = tn(far[0], cg) * scale
    spread_left(dl)
    for b in range(1, sections):
        dw[...] = tn(far[b - 1], g) * scale
        spread_wide(dw, rows)
    dr[...] = tn(c, g) * scale
    spread_wide(dr, rank_rows)
    dl[...] = tn(x, cg) * scale
    spread_left(dl)


def local_kernel(counts, *refs):
    (x, g, near, c, cg, *far), rest = take_pieces(refs, counts)
    sh, sl, wh, wl, lh, ll, rh, rl, *first, out_ref, grad_ref = rest
    last = wh.shape[0] - 1
    out = nn(x, (sh[0], sl[0])) + nn(c, (rh[0], rl[0]))
    for b in range(last):
        out += nn(far[b], (wh[b], wl[b]))
    out_ref[...] = out
    grad = nt(g, (sh[0], sl[0])) + nt(cg, (lh[0], ll[0]))
    grad_ref[...] = grad + nt(near, (wh[last], wl[last]))
    if first:
        ahead_ref, back_ref = first
        count = ahead_ref.shape[0]
        out_ref[:count] += ahead_ref[...]
        grad_ref[:count] += back_ref[...]


def join_kernel(whole_ref, late_ref, out_ref):
    early = whole_ref.shape[0] - late_ref.shape[0]
    out_ref[:early] = whole_ref[:early]
    out_ref[early:] = whole_ref[early:] + late_ref[...]


def place_kernel(sizes, *refs):
    sections, rows, rank_rows, rank, _ = sizes
    bits_ref, self_ref, kept_ref, near_ref, far_ref, w_ref, left_ref, right_ref = refs
    block = kept_ref.shape[1]
    flat = rows * rank // block
    pieces = rows // flat
    w_ref[0, 0] = self_ref[...]
    for s in range(sections):
        chosen = near_ref[:rows]
        for b in range(1, sections):
            chosen = jnp.where(bits_ref[0, s] == b, kept_ref[(b - 1) * rows : b * rows], chosen)
        w_ref[0, 1 + s] = chosen
    at = (sections - 1) * rows
    right_ref[0] = kept_ref[at : at + rank_rows] + near_ref[rows:]
    at += rank_rows
    for p in range(pieces):
        columns = slice(p * rank, (p + 1) * rank)
        left_ref[0, p * flat : (p + 1) * flat, :] = (
            kept_ref[at : at + flat, columns] + far_ref[:, columns]
        )


def on_device(inputs, partner_bits, block_weights, low_left, low_right, cotangent):
    tokens, block = inputs.shape
    sections = partner_bits.shape[1]
    dp_count = lax.axis_size("dp")
    half = dp_count // 2
    rows, rank = low_left.shape[1:]
    rank_rows = low_right.shape[1]
    all_rank = rank_rows * dp_count
    flat = rows * rank // block
    sizes = (sections, rows, rank_rows, rank, dp_count)
    early = tokens * EARLY // 512 // 16 * 16
    late = tokens - early
    lent_rows = rows + rank_rows
    own_rows = sections * rows + rank_rows + flat
    sum_rows = own_rows + lent_rows + flat - rows
    smem = pl.BlockSpec(memory_space=pltpu.SMEM)
    vmem = pl.BlockSpec(memory_space=pltpu.VMEM)
    usual = partner_bits[0, 0] >= 0
    folds = sections == 2
    scale = 1.0 / math.sqrt(tokens * dp_count)

    by_slot = jnp.transpose(block_weights, (0, 2, 1, 3))
    pack_shapes = [(lent_rows + early, block), (flat + early, block), (own_rows - rows, block), (rows, block)]
    out_near, out_far, own, own_self = call(
        pack_kernel,
        [f32(*s) for s in pack_shapes],
        [partner_bits, by_slot, low_left, low_right, inputs, cotangent],
        grid=(1,),
        in_specs=[
            smem, whole(by_slot.shape), whole(low_left.shape), whole(low_right.shape),
            whole((early, block)), whole((early, block)),
        ],
        out_specs=[whole(s) for s in pack_shapes],
        vmem_bytes=PACK_VMEM_BYTES,
    )
    got_near = across(out_near, "feat", 1)
    got_far = across(out_far, "feat", 2)
    own = [own] + [across(own, "dp", k) for k in range(2, dp_count, 2)]
    late_x, got_far = lax.optimization_barrier((inputs[early:], got_far))
    late_far = across(late_x, "feat", 2)
    late_g, got_near = lax.optimization_barrier((cotangent[early:], got_near))
    late_near = across(late_g, "feat", 1)
    early_far, early_near = got_far[flat:], got_near[lent_rows:]
    lent = jnp.concatenate([got_near[:lent_rows], got_far[:flat], own_self])
    lent, own = lax.optimization_barrier((lent, own))
    lent = gather_rows(lent, dp_count)
    *self_keep, self_give = call(
        functools.partial(self_kernel, sizes, scale),
        [f32(rows, block)] * half + [f32(half, rows, block)],
        [inputs, cotangent],
        scratch=[pltpu.VMEM((block, block), F32)],
    )

    s_shape = (1, block, block)
    w_shape = (sections, block, block)
    l_shape = (2, block, rank)
    r_shape = (2, all_rank, block)
    shapes = [s_shape, s_shape, w_shape, w_shape, l_shape, l_shape, r_shape, r_shape]

    def message_shapes(*cuts):
        sends = [(cut, block) for cut in cuts] * sections
        return [(sum(cuts), rank)] * 2 + sends

    made = [b16(*s) for s in shapes]
    if folds:
        made += [f32(*s) for s in message_shapes(early)]

    def prepare(own, lent, keep, give, *early_parts):
        even = jnp.stack([jnp.concatenate(pair) for pair in zip(own, lent)])
        odd = across(even, "dp", 1)
        got = across(give, "dp", 1)
        got, odd = lax.optimization_barrier((got, odd))
        self_grads = keep[0] + got[0]
        for m in range(1, half):
            self_grads = self_grads + across(keep[m] + got[m], "dp", 2 * m)
        operands = [even, odd, *early_parts] if folds else [even, odd]
        return self_grads, *(
            call(
                functools.partial(weights_kernel, sizes),
                made,
                operands,
                grid=(1,),
                in_specs=[whole(even.shape)] * 2 + [whole((early, block))] * (len(operands) - 2),
                out_specs=[whole(s.shape) for s in made],
            )
        )

    def empty(*_):
        return tuple(jnp.zeros(s.shape, s.dtype) for s in [f32(rows, block)] + made)

    self_grads, *weights = lax.cond(
        usual, prepare, empty,
        own, lent, self_keep, self_give, inputs, cotangent, early_far, early_near,
    )
    weights, sent = weights[:8], weights[8:]
    weight_specs = [whole(s) for s in shapes]
    near = [early_near, late_near]
    far = [[early_far, late_far]]
    if folds:
        late_shapes = message_shapes(late)
        step = late // 2 if late % 32 == 0 else late
        late_specs = [by_tokens(step, width) for _, width in late_shapes]
        begun = call(
            begin_kernel,
            [f32(*s) for s in late_shapes],
            [late_x, late_g, *weights[2:]],
            grid=(late // step,),
            in_specs=[by_tokens(step, block)] * 2 + weight_specs[2:],
            out_specs=late_specs,
        )
        late_sent = call(
            messages_kernel,
            [f32(*s) for s in late_shapes],
            [late_far, late_near, *weights[4:], *begun],
            grid=(late // step,),
            in_specs=[by_tokens(step, block)] * 2 + weight_specs[4:] + late_specs,
            out_specs=late_specs,
        )
        first = [across(part, "feat", 1 << b) for b, part in enumerate(sent[2:])]
        rest = list(late_sent[2:])
        rest[1], first = lax.optimization_barrier((rest[1], first))
        first, late_sent = lax.optimization_barrier((first, late_sent))
        rest = [across(part, "feat", 1 << b) for b, part in enumerate(rest)]
        codes, code_grads = ([sent[i], late_sent[i]] for i in range(2))
    else:
        far += [[across(inputs, "feat", 1 << b)] for b in range(2, sections)]
        step = tokens // 2
        wide, thin = by_tokens(step, block), by_tokens(step, rank)
        codes, code_grads = call(
            codes_kernel,
            [f32(tokens, rank)] * 2,
            [inputs, cotangent, jnp.concatenate(far[0]), jnp.concatenate(near), *weights[4:]],
            grid=(2,),
            in_specs=[wide] * 4 + weight_specs[4:],
            out_specs=[thin, thin],
        )
        for b in range(2, sections):
            codes = codes + across(codes, "feat", 1 << b)
            code_grads = code_grads + across(code_grads, "feat", 1 << b)
        messages = call(
            sends_kernel,
            [f32(tokens, block)] * sections,
            [inputs, cotangent, codes, code_grads, *weights[2:]],
            grid=(2,),
            in_specs=[wide, wide, thin, thin, *weight_specs[2:]],
            out_specs=[wide] * sections,
        )
        messages = [across(part, "feat", 1 << b) for b, part in enumerate(messages)]
        codes, code_grads = [codes], [code_grads]

    groups = [[inputs], [cotangent], near, codes, code_grads, *far]
    counts = [len(group) for group in groups]

    def finish(groups, weights, first):
        *keep, give = call(
            functools.partial(grads_kernel, sizes, scale, counts),
            [f32(sum_rows, block)] * half + [f32(half, sum_rows, block)],
            [part for group in groups for part in group],
            scratch=[
                pltpu.VMEM((block, block), F32),
                pltpu.VMEM((all_rank, block), F32),
                pltpu.VMEM((block, rank), F32),
            ],
        )
        groups, give = lax.optimization_barrier((groups, give))
        got = across(give, "dp", 1)
        beside = call(
            functools.partial(local_kernel, counts),
            [f32(tokens, block)] * 2,
            [part for group in groups for part in group] + weights + first,
        )
        total, (out, grad) = scatter_rows([keep[m] + got[m] for m in range(half)], beside)
        at = lent_rows + flat
        return out, grad, total[:lent_rows], total[lent_rows:at], total[at:]

    def nothing(*_):
        shapes = [(tokens, block)] * 2 + [(n, block) for n in (lent_rows, flat, own_rows - rows)]
        return tuple(jnp.zeros(shape, F32) for shape in shapes)

    outputs, grad, near_back, far_back, kept = lax.cond(
        usual, finish, nothing, groups, weights, first if folds else []
    )
    near_back = across(near_back, "feat", 1)
    far_back = across(far_back, "feat", 2)
    if folds:
        outputs, grad = (
            call(join_kernel, [f32(tokens, block)], parts, vmem_bytes=JOIN_VMEM_BYTES)[0]
            for parts in zip((outputs, grad), rest)
        )
    else:
        outputs = outputs + messages[0]
        for part in messages[1:]:
            grad = grad + part
    outputs, grad, kept = lax.optimization_barrier((outputs, grad, kept))
    block_grads, left_grads, right_grads = call(
        functools.partial(place_kernel, sizes),
        [f32(*by_slot.shape), f32(*low_left.shape), f32(*low_right.shape)],
        [partner_bits, self_grads, kept, near_back, far_back],
        grid=(1,),
        in_specs=[smem] + [whole(p.shape) for p in (self_grads, kept, near_back, far_back)],
        out_specs=[whole(by_slot.shape), whole(low_left.shape), whole(low_right.shape)],
    )
    block_grads = jnp.transpose(block_grads, (0, 2, 1, 3))
    return (outputs, grad, block_grads, left_grads, right_grads)


def solution(mesh):
    in_specs = (
        P("dp", "feat"),
        P("feat", None),
        P("feat", "dp", None, None),
        P("feat", "dp", None),
        P("feat", "dp", None),
        P("dp", "feat"),
    )
    out_specs = (
        P("dp", "feat"),
        P("dp", "feat"),
        P("feat", "dp", None, None),
        P("feat", "dp", None),
        P("feat", "dp", None),
    )
    return jax.shard_map(
        on_device, mesh=mesh, in_specs=in_specs, out_specs=out_specs, check_vma=False
    )
```
